32 devices in a mesh: rows: 8 (over z, y), keys: 4 (over x, core).
Axes of the slice: x: 2, y: 2, z: 4, core: 2. Of those that a mesh axis runs over, the one named last changes fastest.
Arguments:
- activations: bfloat16 [8, 896, 1024], P('rows', 'keys'), may hold values from -6 to 6
- segments: int32 [8, 896], P('rows'), may hold values from 0 to 15, never falling along the last dimension, each value on 1 to 256 neighbouring positions
- prefix_keys: bfloat16 [2, 64, 1024], P(None, 'keys'), may hold values from -6 to 6
- prefix_values: bfloat16 [2, 64, 1024], P(None, 'keys'), may hold values from -6 to 6
- w_query: bfloat16 [2, 1024, 1024], P(None, 'rows'), may hold values from -0.1875 to 0.1875
- w_key: bfloat16 [2, 1024, 1024], P(None, 'rows'), may hold values from -0.1875 to 0.1875
- w_value: bfloat16 [2, 1024, 1024], P(None, 'rows'), may hold values from -0.1875 to 0.1875
- w_out: bfloat16 [2, 1024, 1024], P(None, 'rows'), may hold values from -1.5 to 1.5
- w_up: bfloat16 [2, 1024, 4096], P(None, 'rows'), may hold values from -0.1875 to 0.1875
- ff_bias: float32 [2, 4096], replicated, may hold values from -3 to 3
- w_down: bfloat16 [2, 4096, 1024], P(None, 'rows'), may hold values from -0.09375 to 0.09375
- ln_gain: float32 [2, 2, 1024], replicated, may hold values from 0.5 to 1.5
- ln_bias: float32 [2, 2, 1024], replicated, may hold values from -1.2 to 1.2
- cotangent: bfloat16 [8, 896, 1024], P('rows', 'keys'), may hold values from -6 to 6
Outputs:
- block_output: bfloat16 [8, 896, 1024], P('rows', 'keys')
- input_grad: float32 [8, 896, 1024], P('rows', 'keys')
- prefix_key_grad: float32 [2, 64, 1024], P(None, 'keys')
- prefix_value_grad: float32 [2, 64, 1024], P(None, 'keys')
The draws below stay inside these ranges and needn't reach their ends.
Inputs may be any that keep to these rules, and one draw needn't show every extreme that they name: `segments`: along each row the pair ids never fall, each pair covers 1 to 256 positions, and one pair of each row covers exactly 256.
All inputs are finite; a program needn't handle non-finite values.
Results may differ from the reference program's by a relative error of at most 0.025.
Values may be sent and summed in bfloat16 or wider, within the bound.
No kernel may reach another device: no remote copies, remote signals or barrier semaphores. Data moves between devices by JAX's collectives and lax.ppermute only.
A program may use at most 256 MiB of HBM per device.

```python
import math
import jax
import jax.numpy as jnp
import numpy as np
from jax import lax

D = 1024
H = 16
HD = 64
FF = 4096
PREFIX = 64
LAYERS = 2
L = 896
SEGS = 16
MOST = 256
ROWS = 8


def level_of(rng, extent, cuts, smallest, high):
    factor_of, own = 1.0, jax.random.fold_in(rng, 6)
    for axis_at, parts in cuts:
        draws = jnp.exp(jax.random.uniform(jax.random.fold_in(own, axis_at), (parts,), jnp.float32, smallest / len(cuts), high / len(cuts)))
        factor_of = factor_of * jnp.repeat(draws, extent[axis_at] // parts).reshape([-1 if axis == axis_at else 1 for axis in range(len(extent))])
    return factor_of


def length_profile(amount, total, limit, lean):
    portions = [(1 << 20) // math.isqrt(grade ** lean) + 1 for grade in range(2, amount + 1)]
    spare, holding = total - limit - (amount - 1), [1] * (amount - 1)
    while spare > 0:
        candidates = [i for i in range(amount - 1) if holding[i] < limit]
        pool, budget = sum([portions[i] for i in candidates]), spare
        for i in candidates:
            extra = min(limit - holding[i], max(1, budget * portions[i] // pool), spare)
            holding[i] = holding[i] + extra
            spare = spare - extra
    return np.array([limit] + holding)


def uneven(rng, number_of, total, limit, lean):
    if number_of == 2:
        one = jax.random.randint(rng, (), max(1, total - limit), min(limit, total - 1) + 1)
        return jnp.stack([one, total - one])
    sizes = jnp.asarray(length_profile(number_of, total, limit, lean), jnp.int32)
    twos = (number_of - 1) // 2
    donor, receiver = sizes[1:1 + 2 * twos:2], sizes[2:2 + 2 * twos:2]
    room = jnp.minimum(donor - 1, limit - receiver)
    passed = jax.random.randint(jax.random.fold_in(rng, 1), (twos,), 0, 1 << 20) % (room + 1)
    sizes = sizes.at[1:1 + 2 * twos:2].set(donor - passed).at[2:2 + 2 * twos:2].set(receiver + passed)
    return sizes[jax.random.permutation(jax.random.fold_in(rng, 2), number_of)]


def scatter_about(key, shape, scale, most, shards=(), kind=jnp.bfloat16):
    drawn = jax.random.normal(key, shape, jnp.float32) * scale
    if len(shards) > 0:
        drawn = level_of(key, shape, shards, -0.22, 0.18) * drawn
    return jnp.clip(drawn, min=-most, max=most).astype(kind)


def setup_inputs(seed: int = 0) -> dict:
    seeds = jax.random.split(jax.random.key(seed), 15)
    activations = scatter_about(seeds[0], (ROWS, L, D), 1.0, 6.0, ((0, 8), (1, 4)))
    segments = jax.vmap(lambda own: jnp.searchsorted(jnp.cumsum(uneven(own, SEGS, L, MOST, 2)), jnp.arange(L), side="right"))(jax.random.split(seeds[1], ROWS)).reshape((ROWS, L)).astype(jnp.int32)
    prefix_keys = scatter_about(seeds[2], (LAYERS, PREFIX, D), 1.0, 6.0, ((1, 4),))
    prefix_values = scatter_about(seeds[3], (LAYERS, PREFIX, D), 1.0, 6.0, ((1, 4),))
    w_query = scatter_about(seeds[4], (LAYERS, D, D), D ** -0.5, 0.1875, ((1, 8),))
    w_key = scatter_about(seeds[5], (LAYERS, D, D), D ** -0.5, 0.1875, ((1, 8),))
    w_value = scatter_about(seeds[6], (LAYERS, D, D), D ** -0.5, 0.1875, ((1, 8),))
    w_out = scatter_about(seeds[7], (LAYERS, D, D), (D // 64) ** -0.5, 1.5, ((1, 8),))
    w_up = scatter_about(seeds[8], (LAYERS, D, FF), D ** -0.5, 0.1875, ((1, 8),))
    ff_bias = scatter_about(seeds[9], (LAYERS, FF), 0.5, 3.0, (), jnp.float32)
    w_down = scatter_about(seeds[10], (LAYERS, FF, D), FF ** -0.5, 0.09375, ((1, 8),))
    ln_gain = jnp.clip(1.0 + 0.1 * jax.random.normal(seeds[11], (LAYERS, 2, D), jnp.float32), 0.5, 1.5)
    ln_bias = scatter_about(seeds[12], (LAYERS, 2, D), 0.2, 1.2, (), jnp.float32)
    cotangent = scatter_about(seeds[13], (ROWS, L, D), 1.0, 6.0, ((0, 8), (1, 4)))
    return {"activations": activations, "segments": segments, "prefix_keys": prefix_keys, "prefix_values": prefix_values, "w_query": w_query, "w_key": w_key, "w_value": w_value, "w_out": w_out, "w_up": w_up, "ff_bias": ff_bias, "w_down": w_down, "ln_gain": ln_gain, "ln_bias": ln_bias, "cotangent": cotangent}


NORM_EPSILON = 1e-05
MASKED_SCORE = -1000000000.0
SCORE_SCALE = 0.125

@jax.custom_vjp
def low(v):
    return lax.optimization_barrier(v.astype(jnp.bfloat16)).astype(jnp.float32)

@jax.custom_vjp
def low_back(v):
    return v

def low_keep(v):
    return (low(v), None)

def low_pass(kept, grad):
    return (grad,)

def back_keep(v):
    return (v, None)

def back_low(kept, grad):
    return (low(grad),)
low.defvjp(low_keep, low_pass)
low_back.defvjp(back_keep, back_low)

def matmul(left, right):
    return jnp.dot(left, right, precision=lax.Precision.HIGHEST)

def layer_norm(hidden, gain, shift):
    centered = hidden - lax.optimization_barrier(jnp.mean(hidden, -1, keepdims=True))
    return centered * lax.rsqrt(lax.optimization_barrier(jnp.mean(centered * centered, -1, keepdims=True)) + NORM_EPSILON) * gain + shift

def row_layer(inputs, row_segments, prefix_key, prefix_value, query_weight, key_weight, value_weight, out_weight, up_weight, up_bias, down_weight, gain_pair, shift_pair):
    inputs_low = low(inputs)
    queries = low(low_back(SCORE_SCALE * matmul(inputs_low, query_weight)))
    keys_local = low(low_back(matmul(inputs_low, key_weight)))
    values_local = low(low_back(matmul(inputs_low, value_weight)))
    key_rows = jnp.concatenate([keys_local, prefix_key], 0)
    value_rows = jnp.concatenate([values_local, prefix_value], 0)
    scores = jnp.einsum('qhd,khd->hqk', queries.reshape(L, H, HD), key_rows.reshape(L + PREFIX, H, HD), precision=lax.Precision.HIGHEST)
    scores = low_back(scores)
    allowed = jnp.concatenate([row_segments[:, None] == row_segments[None, :], jnp.ones((L, PREFIX), dtype=bool)], 1)
    scores = jnp.where(allowed[None], scores, MASKED_SCORE)
    attend = low(jax.nn.softmax(scores, axis=-1))
    attended = jnp.einsum('hqk,khd->qhd', attend, value_rows.reshape(L + PREFIX, H, HD), precision=lax.Precision.HIGHEST).reshape(L, D)
    attended = low(low_back(attended))
    middle = layer_norm(inputs + low_back(matmul(attended, out_weight)), gain_pair[0], shift_pair[0])
    pre_gelu = low_back(matmul(low(middle), up_weight) + up_bias)
    activated = low(jax.nn.gelu(pre_gelu, approximate=False))
    return layer_norm(middle + low_back(matmul(activated, down_weight)), gain_pair[1], shift_pair[1])

def reference(activations, segments, prefix_keys, prefix_values, w_query, w_key, w_value, w_out, w_up, ff_bias, w_down, ln_gain, ln_bias, cotangent):
    query_all = w_query.astype(jnp.float32)
    key_all = w_key.astype(jnp.float32)
    value_all = w_value.astype(jnp.float32)
    out_all = w_out.astype(jnp.float32)
    up_all = w_up.astype(jnp.float32)
    down_all = w_down.astype(jnp.float32)
    row_step = jax.checkpoint(row_layer)

    def forward(inputs, key_table, value_table):
        for layer_index in range(LAYERS):
            inputs = lax.map(lambda packed: row_step(packed[0], packed[1], key_table[layer_index], value_table[layer_index], query_all[layer_index], key_all[layer_index], value_all[layer_index], out_all[layer_index], up_all[layer_index], ff_bias[layer_index], down_all[layer_index], ln_gain[layer_index], ln_bias[layer_index]), (inputs, segments))
        return inputs
    output, backward = jax.vjp(forward, activations.astype(jnp.float32), prefix_keys.astype(jnp.float32), prefix_values.astype(jnp.float32))
    input_grad, key_grad, value_grad = backward(cotangent.astype(jnp.float32))
    return (output.astype(jnp.bfloat16), input_grad, key_grad, value_grad)
```

```python
from functools import partial

import jax
import jax.numpy as jnp
import numpy as np
from jax import lax
from jax.experimental import pallas as pl
from jax.experimental.pallas import tpu as pltpu
from jax.sharding import PartitionSpec as P

H = 16
HD = 64
LAYERS = 2
PAIRS = H // 2
EDGE = 32
LANES = 256
NORM_EPSILON = 1e-05
MASKED_SCORE = -1000000000.0
SCORE_SCALE = 0.125
F32 = jnp.float32
BF16 = jnp.bfloat16
MIB = 1 << 20


def nn(a, b):
    return lax.dot_general(a, b, (((1,), (0,)), ((), ())), preferred_element_type=F32)


def nt(a, b):
    return lax.dot_general(a, b, (((1,), (1,)), ((), ())), preferred_element_type=F32)


def ds(start, size):
    return pl.ds(pl.multiple_of(start, size), size)


def layer_norm(hidden, gain, shift):
    centered = hidden - jnp.mean(hidden, -1, keepdims=True)
    inverse = lax.rsqrt(jnp.mean(centered * centered, -1, keepdims=True) + NORM_EPSILON)
    normed = centered * inverse
    return normed * gain + shift, normed, inverse


def norm_back(grad_out, gain, normed, inverse):
    scaled = grad_out * gain
    return inverse * (
        scaled
        - jnp.mean(scaled, -1, keepdims=True)
        - normed * jnp.mean(scaled * normed, -1, keepdims=True)
    )


def start_loads(table, pieces, weights, sems):
    at = 0
    for piece in pieces:
        blocks, rows, width = piece.shape

        def start(i, carry, piece=piece, at=at, rows=rows, width=width):
            row = table[at + i]

            @pl.when(row >= 0)
            def _():
                pltpu.make_async_copy(
                    piece.at[i], weights.at[ds(row, rows)], sems.at[row // width]
                ).start()

            return carry

        lax.fori_loop(0, blocks, start, 0)
        at += blocks


def wait_load(weights, sems, index):
    width = weights.shape[1]
    part = weights.at[pl.ds(index * width, width)]
    pltpu.make_async_copy(part, part, sems.at[index]).wait()


def pair_blocks(half):
    zero = jnp.zeros((HD, LANES), half.dtype)
    return jnp.concatenate(
        [
            jnp.concatenate([half[:HD], zero], 1),
            jnp.concatenate([zero, half[HD:]], 1),
        ],
        0,
    )


def attention_kernel(count, *refs):
    (table, own, near, across, edge, residual, bias, prefix_k, prefix_v, gain, shift) = refs[:11]
    pieces = refs[11 : 11 + count]
    (middle, normed, inverse, query_t, value8, key_t, attend, heads_t) = refs[11 + count : 19 + count]
    (weights, window, key8, value_t, scores, sems) = refs[19 + count :]
    tokens, width = own.shape
    span = window.shape[0]
    keys = key8.shape[1]
    start_loads(table, pieces, weights, sems)
    window[pl.ds(0, tokens)] = own[...]
    window[pl.ds(tokens, tokens)] = near[...]
    window[pl.ds(2 * tokens, tokens)] = across[...]
    window[pl.ds(3 * tokens, EDGE)] = edge[...]
    pad = jnp.zeros((LANES - tokens, 256), BF16)
    for index in range(3):
        wait_load(weights, sems, index)

    def tile(j, carry):
        columns = ds(j * 256, 256)
        query = (SCORE_SCALE * nn(own[...], weights[pl.ds(0, width), columns])).astype(BF16)
        query_t[columns, :] = jnp.concatenate([query, pad], 0).T
        for row, prefix, split, turned in ((width, prefix_k, key8, key_t), (2 * width, prefix_v, value8, value_t)):
            local = nn(window[...], weights[pl.ds(row, width), columns]).astype(BF16)
            whole = jnp.concatenate([local, prefix[:, columns]], 0)
            split[2 * j] = whole[:, :128]
            split[2 * j + 1] = whole[:, 128:]
            turned[columns, :] = whole.T
        return carry

    lax.fori_loop(0, width // 256, tile, 0)
    wide = jnp.zeros((1, 2 * LANES), F32)
    step = 128

    def pair(p, carry):
        blocks = pair_blocks(query_t[ds(p * 128, 128), :])
        top = wide + 2 * MASKED_SCORE
        for c in range(0, keys, step):
            part = nn(key8[p, pl.ds(c, step), :], blocks)
            mask = bias[pl.ds(c, step), :]
            part = part + jnp.concatenate([mask, mask], 1)
            scores[pl.ds(c, step), :] = part
            top = jnp.maximum(top, jnp.max(part, 0, keepdims=True))
        total = wide
        for c in range(0, keys, step):
            part = jnp.exp(scores[pl.ds(c, step), :] - top)
            scores[pl.ds(c, step), :] = part
            total = total + jnp.sum(part, 0, keepdims=True)
        scale = 1.0 / total
        for c in range(0, keys, step):
            attend[p, pl.ds(c, step), :] = (scores[pl.ds(c, step), :] * scale).astype(BF16)
        for half in range(2):
            rows = pl.ds(pl.multiple_of(p * 128 + half * HD, HD), HD)
            heads_t[rows, :] = nn(value_t[rows, :], attend[p, :, pl.ds(half * LANES, LANES)])
        return carry

    lax.fori_loop(0, PAIRS, pair, 0)
    wait_load(weights, sems, 3)
    heads = heads_t[...].astype(BF16).T[:tokens]

    def out(j, carry):
        columns = ds(j * 256, 256)
        middle[:, columns] = residual[:, columns] + nn(heads, weights[pl.ds(3 * width, width), columns])
        return carry

    lax.fori_loop(0, width // 256, out, 0)
    result, n, r = layer_norm(middle[...], gain[...], shift[...])
    middle[...] = result
    normed[...] = n
    inverse[...] = r


def forward_kernel(count, *refs):
    (table, middle, up_bias, gain, shift) = refs[:5]
    pieces = refs[5 : 5 + count]
    (output, low, normed, inverse, slope) = refs[5 + count : 10 + count]
    (weights, middle_low, hidden, sems) = refs[10 + count :]
    tokens, width = middle.shape
    wide = up_bias.shape[1]
    start_loads(table, pieces, weights, sems)
    middle_low[...] = middle[...].astype(BF16)
    for block in range(wide // width):
        wait_load(weights, sems, block)

        def tile(j, carry, block=block):
            columns = ds(j * 256, 256)
            place = ds(block * width + j * 256, 256)
            u = nn(middle_low[...], weights[pl.ds(block * width, width), columns]) + up_bias[:, place]
            part = 0.5 + 0.5 * lax.erf(u * (0.5**0.5))
            hidden[:, place] = (u * part).astype(BF16)
            slope[:, place] = (part + u * (jnp.exp(-0.5 * u * u) * ((2 * np.pi) ** -0.5))).astype(BF16)
            return carry

        lax.fori_loop(0, width // 256, tile, 0)
    for block in range(wide // width):
        wait_load(weights, sems, wide // width + block)

    def down(j, carry):
        columns = ds(j * 256, 256)
        output[:, columns] = middle[:, columns] + nn(hidden[...], weights[pl.ds(wide, wide), columns])
        return carry

    lax.fori_loop(0, width // 256, down, 0)
    result, n, r = layer_norm(output[...], gain[...], shift[...])
    output[...] = result
    low[...] = result.astype(BF16)
    normed[...] = n
    inverse[...] = r


def forward_back_kernel(count, *refs):
    (table, grad, normed_two, inverse_two, gain_two, slope, normed_one, inverse_one, gain_one) = refs[:9]
    pieces = refs[9 : 9 + count]
    (grad_one, heads_grad) = refs[9 + count : 11 + count]
    (weights, low, hidden, sems) = refs[11 + count :]
    tokens, width = grad.shape
    wide = slope.shape[1]
    many = wide // width
    start_loads(table, pieces, weights, sems)
    grad_two = norm_back(grad[...], gain_two[...], normed_two[...], inverse_two[...])
    grad_one[...] = grad_two
    low[pl.ds(0, tokens), :] = grad_two.astype(BF16)
    low[pl.ds(tokens, LANES - tokens), :] = jnp.zeros((LANES - tokens, width), BF16)
    for block in range(many):
        wait_load(weights, sems, many + block)

        def tile(j, carry, block=block):
            place = ds(block * width + j * 256, 256)
            back = nt(low[pl.ds(0, tokens), :], weights[pl.ds(pl.multiple_of(wide + block * width + j * 256, 256), 256), :])
            hidden[:, place] = (back * slope[:, place].astype(F32)).astype(BF16)
            return carry

        lax.fori_loop(0, width // 256, tile, 0)
    for block in range(many):
        wait_load(weights, sems, block)

    def up(j, carry):
        columns = ds(j * 256, 256)
        total = grad_one[:, columns]
        for block in range(many):
            rows = pl.ds(pl.multiple_of(block * width + j * 256, 256), 256)
            total = total + nt(hidden[:, pl.ds(block * width, width)], weights[rows, :])
        grad_one[:, columns] = total
        return carry

    lax.fori_loop(0, width // 256, up, 0)
    back = norm_back(grad_one[...], gain_one[...], normed_one[...], inverse_one[...])
    grad_one[...] = back
    low[pl.ds(0, tokens), :] = back.astype(BF16)
    wait_load(weights, sems, 2 * many)

    def out(j, carry):
        rows = ds(j * 256, 256)
        place = pl.ds(pl.multiple_of(2 * wide + j * 256, 256), 256)
        heads_grad[rows, :] = nt(weights[place, :], low[...]).astype(BF16)
        return carry

    lax.fori_loop(0, width // 256, out, 0)


def attention_back_kernel(count, *refs):
    (table, heads_grad, heads_t, query_t, value8, key_t, attend_hbm) = refs[:7]
    pieces = refs[7 : 7 + count]
    (query_grad, key_own, value_own, halo, prefix_grad) = refs[7 + count : 12 + count]
    (weights, attend, key_grad, value_grad, query_grad_t, steps, sems, attend_sems) = refs[12 + count :]
    tokens, width = query_grad.shape
    keys = attend.shape[1]
    prefix = prefix_grad.shape[1]
    span = keys - prefix
    for p in range(PAIRS):
        pltpu.make_async_copy(attend_hbm.at[p], attend.at[p], attend_sems.at[p]).start()
    start_loads(table, pieces, weights, sems)
    step = 128

    def pair(p, carry):
        pltpu.make_async_copy(attend_hbm.at[p], attend.at[p], attend_sems.at[p]).wait()
        rows = ds(p * 128, 128)
        grad_t = heads_grad[rows, :]
        product = grad_t.astype(F32) * heads_t[rows, :]
        dots = jnp.concatenate(
            [jnp.sum(product[:HD], 0, keepdims=True), jnp.sum(product[HD:], 0, keepdims=True)], 1
        )
        blocks = pair_blocks(grad_t)
        for c in range(0, keys, step):
            part = nn(value8[p, pl.ds(c, step), :], blocks) - dots
            steps[pl.ds(c, step), :] = (attend[p, pl.ds(c, step), :].astype(F32) * part).astype(BF16)
        columns = ds(p * 128, 128)
        grad_v = nt(attend[p], blocks)
        value_grad[:, columns] = grad_v.astype(BF16)
        prefix_grad[1, :, columns] = grad_v[span:]
        grad_k = nt(steps[...], pair_blocks(query_t[rows, :]))
        key_grad[:, columns] = grad_k.astype(BF16)
        prefix_grad[0, :, columns] = grad_k[span:]
        for half in range(2):
            place = pl.ds(pl.multiple_of(p * 128 + half * HD, HD), HD)
            query_grad_t[place, :] = nn(key_t[place, :], steps[:, pl.ds(half * LANES, LANES)]).astype(BF16)
        return carry

    lax.fori_loop(0, PAIRS, pair, 0)
    query_grad[...] = query_grad_t[...].T[:tokens]
    key_own[...] = key_grad[pl.ds(0, tokens), :]
    value_own[...] = value_grad[pl.ds(0, tokens), :]
    wait_load(weights, sems, 0)
    wait_load(weights, sems, 1)

    def outer(j, carry):
        columns = ds(j * 256, 256)
        place = pl.ds(pl.multiple_of(width + j * 256, 256), 256)
        halo[:, columns] = (
            nt(key_grad[pl.ds(tokens, span - tokens), :], weights[columns, :])
            + nt(value_grad[pl.ds(tokens, span - tokens), :], weights[place, :])
        ).astype(BF16)
        return carry

    lax.fori_loop(0, width // 256, outer, 0)


def input_back_kernel(count, *refs):
    (table, grad_one, query_grad, key_own, value_own) = refs[:5]
    pieces = refs[5 : 5 + count]
    grad_input = refs[5 + count]
    (weights, sems) = refs[6 + count :]
    width = grad_one.shape[1]
    start_loads(table, pieces, weights, sems)
    for index in range(3):
        wait_load(weights, sems, index)

    def tile(j, carry):
        columns = ds(j * 256, 256)
        rows = [pl.ds(pl.multiple_of(i * width + j * 256, 256), 256) for i in range(3)]
        grad_input[:, columns] = (
            grad_one[:, columns]
            + SCORE_SCALE * nt(query_grad[...], weights[rows[0], :])
            + nt(key_own[...], weights[rows[1], :])
            + nt(value_own[...], weights[rows[2], :])
        )
        return carry

    lax.fori_loop(0, width // 256, tile, 0)


VMEM = pl.BlockSpec(memory_space=pltpu.VMEM)
SMEM = pl.BlockSpec(memory_space=pltpu.SMEM)
ANY = pl.BlockSpec(memory_space=pl.ANY)


def call(kernel, table, operands, kept, pieces, outs, scratch, limit, flops, any_outs=()):
    moved = sum(x.size * x.dtype.itemsize for x in pieces) + sum(x.size * x.dtype.itemsize for x in operands)
    return pl.pallas_call(
        partial(kernel, len(pieces)),
        out_shape=outs,
        in_specs=[SMEM] + [VMEM] * len(operands) + [ANY] * (len(kept) + len(pieces)),
        out_specs=[ANY if i in any_outs else VMEM for i in range(len(outs))],
        scratch_shapes=scratch,
        compiler_params=pltpu.CompilerParams(vmem_limit_bytes=limit * MIB),
        cost_estimate=pl.CostEstimate(flops=flops, bytes_accessed=moved, transcendentals=0),
    )(table, *operands, *kept, *pieces)


def shape(*sizes, dtype=BF16):
    return jax.ShapeDtypeStruct(sizes, dtype)


def attention_forward(inputs, inputs_low, around, bias, prefix_k, prefix_v, gain, shift, table, pieces):
    tokens, width = inputs.shape
    keys = bias.shape[0]
    span = keys - prefix_k.shape[0]
    return call(
        attention_kernel,
        table,
        [inputs_low, *around, inputs, bias, prefix_k, prefix_v, gain, shift],
        [],
        pieces,
        [
            shape(tokens, width, dtype=F32),
            shape(tokens, width, dtype=F32),
            shape(tokens, 1, dtype=F32),
            shape(width, LANES),
            shape(PAIRS, keys, 128),
            shape(width, keys),
            shape(PAIRS, keys, 2 * LANES),
            shape(width, LANES, dtype=F32),
        ],
        [
            pltpu.VMEM((4 * width, width), BF16),
            pltpu.VMEM((span, width), BF16),
            pltpu.VMEM((PAIRS, keys, 128), BF16),
            pltpu.VMEM((width, keys), BF16),
            pltpu.VMEM((keys, 2 * LANES), F32),
            pltpu.SemaphoreType.DMA((4,)),
        ],
        40,
        2 * tokens * width * width * 8,
    )


def feed_forward(middle, up_bias, gain, shift, table, pieces):
    tokens, width = middle.shape
    wide = up_bias.shape[1]
    many = wide // width
    return call(
        forward_kernel,
        table,
        [middle, up_bias, gain, shift],
        [],
        pieces,
        [
            shape(tokens, width, dtype=F32),
            shape(tokens, width),
            shape(tokens, width, dtype=F32),
            shape(tokens, 1, dtype=F32),
            shape(tokens, wide),
        ],
        [
            pltpu.VMEM((2 * wide, width), BF16),
            pltpu.VMEM((tokens, width), BF16),
            pltpu.VMEM((tokens, wide), BF16),
            pltpu.SemaphoreType.DMA((2 * many,)),
        ],
        40,
        4 * tokens * width * wide,
    )


def feed_back(grad, saved_two, gain_two, slope, saved_one, gain_one, table, pieces):
    tokens, width = grad.shape
    wide = slope.shape[1]
    many = wide // width
    return call(
        forward_back_kernel,
        table,
        [grad, *saved_two, gain_two, slope, *saved_one, gain_one],
        [],
        pieces,
        [shape(tokens, width, dtype=F32), shape(width, LANES)],
        [
            pltpu.VMEM((2 * wide + width, width), BF16),
            pltpu.VMEM((LANES, width), BF16),
            pltpu.VMEM((tokens, wide), BF16),
            pltpu.SemaphoreType.DMA((2 * many + 1,)),
        ],
        40,
        4 * tokens * width * wide + 2 * tokens * width * width,
    )


def attention_back(heads_grad, heads_t, query_t, value8, key_t, attend, tokens, prefix, table, pieces):
    width = heads_grad.shape[0]
    keys = attend.shape[1]
    span = keys - prefix
    return call(
        attention_back_kernel,
        table,
        [heads_grad, heads_t, query_t, value8, key_t],
        [attend],
        pieces,
        [
            shape(tokens, width),
            shape(tokens, width),
            shape(tokens, width),
            shape(span - tokens, width),
            shape(2, prefix, width, dtype=F32),
        ],
        [
            pltpu.VMEM((2 * width, width), BF16),
            pltpu.VMEM(attend.shape, BF16),
            pltpu.VMEM((keys, width), BF16),
            pltpu.VMEM((keys, width), BF16),
            pltpu.VMEM((width, LANES), BF16),
            pltpu.VMEM((keys, 2 * LANES), BF16),
            pltpu.SemaphoreType.DMA((2,)),
            pltpu.SemaphoreType.DMA((PAIRS,)),
        ],
        40,
        2 * tokens * width * keys * 8,
    )


def input_back(grad_one, query_grad, key_own, value_own, table, pieces):
    tokens, width = grad_one.shape
    return call(
        input_back_kernel,
        table,
        [grad_one, query_grad, key_own, value_own],
        [],
        pieces,
        [shape(tokens, width, dtype=F32)],
        [pltpu.VMEM((3 * width, width), BF16), pltpu.SemaphoreType.DMA((3,))],
        30,
        6 * tokens * width * width,
    )[0]


def xor_pairs(count, bit):
    return [(i, i ^ bit) for i in range(count)]


def body(
    activations,
    segments,
    prefix_keys,
    prefix_values,
    w_query,
    w_key,
    w_value,
    w_out,
    w_up,
    ff_bias,
    w_down,
    ln_gain,
    ln_bias,
    cotangent,
):
    _, tokens, width = activations.shape
    wide = w_up.shape[2]
    ratio = wide // width
    places = lax.axis_size("keys")
    parts = lax.axis_size("rows")
    rows = width // parts
    place = lax.axis_index("keys")
    prefix = prefix_keys.shape[1] * places
    first_half = place < places // 2

    def blocks_of(layer):
        up = [w_up[layer][:, i * width : (i + 1) * width] for i in range(ratio)]
        down = [w_down[layer][i * rows : (i + 1) * rows] for i in range(ratio)]
        return (
            jnp.stack([w_query[layer], w_key[layer], w_value[layer], w_out[layer]]),
            jnp.stack(up + down),
        )

    def gather(blocks):
        share = blocks.shape[0] // places
        own = lax.dynamic_slice_in_dim(blocks, place * share, share, 0)
        return [lax.all_gather(own, ("rows", "keys"), axis=0, tiled=True)]

    packs = [blocks_of(layer) for layer in range(LAYERS)]
    groups = [[gather(part) for part in pack] for pack in packs]

    owner = np.repeat(np.arange(parts), 4)
    kind = np.tile(np.arange(4), parts)
    attention_rows = kind * width + owner * rows
    owner = np.repeat(np.arange(parts), 2 * ratio)
    part = np.tile(np.arange(2 * ratio), parts)
    feed_rows = np.where(
        part < ratio,
        part * width + owner * rows,
        wide + owner * rows * ratio + (part - ratio) * rows,
    )

    def only(*kinds):
        table = np.full(4 * parts, -1)
        for i, which in enumerate(kinds):
            table = np.where(kind == which, attention_rows + (i - which) * width, table)
        return table

    def as_table(values):
        return jnp.asarray(values, jnp.int32)

    def exchange(low):
        near = lax.ppermute(low, "keys", xor_pairs(places, 1))
        across = lax.ppermute(low, "keys", [(1, 2), (2, 1)])
        edge = lax.ppermute(
            jnp.where(first_half, low[tokens - EDGE :], low[:EDGE]), "keys", xor_pairs(places, 2)
        )
        return near, across, edge

    line = segments[0]

    def ids(where, start, size):
        return lax.dynamic_slice_in_dim(line, where * tokens + start, size, 0)

    own_ids = ids(place, 0, tokens)
    across_ids = jnp.where(
        (place == 1) | (place == 2), ids(jnp.clip(3 - place, 0, places - 1), 0, tokens), -1
    )
    edge_ids = ids(place ^ 2, jnp.where(first_half, 0, tokens - EDGE), EDGE)
    key_ids = jnp.concatenate([own_ids, ids(place ^ 1, 0, tokens), across_ids, edge_ids])
    allowed = jnp.concatenate([key_ids[:, None] == own_ids[None, :], jnp.ones((prefix, tokens), bool)], 0)
    bias = jnp.pad(jnp.where(allowed, 0.0, MASKED_SCORE).astype(F32), ((0, 0), (0, LANES - tokens)))

    prefixes = lax.all_gather(jnp.stack([prefix_keys, prefix_values]), "keys", axis=2, tiled=True)

    low = activations[0]
    hidden = low.astype(F32)
    saved = []
    for layer in range(LAYERS):
        gains, shifts = ln_gain[layer][:, None], ln_bias[layer][:, None]
        around = exchange(low)
        middle, normed_one, inverse_one, query_t, value8, key_t, attend, heads_t = attention_forward(
            hidden,
            low,
            around,
            bias,
            prefixes[0, layer],
            prefixes[1, layer],
            gains[0],
            shifts[0],
            as_table(attention_rows),
            groups[layer][0],
        )
        hidden, low, normed_two, inverse_two, slope = feed_forward(
            middle, ff_bias[layer][None], gains[1], shifts[1], as_table(feed_rows), groups[layer][1]
        )
        saved.append(
            ((normed_one, inverse_one), (normed_two, inverse_two), slope, heads_t, query_t, value8, key_t, attend)
        )
    result = low

    gradient = cotangent[0].astype(F32)
    prefix_parts = [None] * LAYERS
    for layer in range(LAYERS - 1, -1, -1):
        saved_one, saved_two, slope, heads_t, query_t, value8, key_t, attend = saved[layer]
        gains = ln_gain[layer][:, None]
        grad_one, heads_grad = feed_back(
            gradient,
            saved_two,
            gains[1],
            slope,
            saved_one,
            gains[0],
            as_table(np.concatenate([feed_rows, only(3) + 2 * wide * (only(3) >= 0)])),
            groups[layer][1] + groups[layer][0],
        )
        query_grad, key_own, value_own, halo, prefix_grad = attention_back(
            heads_grad, heads_t, query_t, value8, key_t, attend, tokens, prefix, as_table(only(1, 2)), groups[layer][0]
        )
        near = lax.ppermute(halo[:tokens], "keys", xor_pairs(places, 1))
        across = lax.ppermute(halo[tokens : 2 * tokens], "keys", [(1, 2), (2, 1)])
        edge = lax.ppermute(halo[2 * tokens :], "keys", xor_pairs(places, 2)).astype(F32)
        gradient = input_back(grad_one, query_grad, key_own, value_own, as_table(only(0, 1, 2)), groups[layer][0])
        lead = jnp.where(first_half, 0.0, edge)
        tail = jnp.where(first_half, edge, 0.0)
        gradient = (
            gradient
            + near.astype(F32)
            + across.astype(F32)
            + jnp.concatenate([lead, jnp.zeros((tokens - 2 * EDGE, width), F32), tail], 0)
        )
        share = prefix // places
        split = prefix_grad.reshape(2, places, share, width).transpose(1, 0, 2, 3)
        split = lax.all_to_all(split, "keys", 0, 0)
        prefix_parts[layer] = lax.psum(jnp.sum(split, 0).astype(BF16), "rows").astype(F32)
    return (
        result[None],
        gradient[None],
        jnp.stack([part[0] for part in prefix_parts]),
        jnp.stack([part[1] for part in prefix_parts]),
    )


def solution(mesh):
    placed = (
        P("rows", "keys", None),
        P("rows", None),
        P(None, "keys", None),
        P(None, "keys", None),
        P(None, "rows", None),
        P(None, "rows", None),
        P(None, "rows", None),
        P(None, "rows", None),
        P(None, "rows", None),
        P(),
        P(None, "rows", None),
        P(),
        P(),
        P("rows", "keys", None),
    )
    return jax.shard_map(
        body,
        mesh=mesh,
        in_specs=placed,
        out_specs=(
            P("rows", "keys", None),
            P("rows", "keys", None),
            P(None, "keys", None),
            P(None, "keys", None),
        ),
        check_vma=False,
    )
```

```python
from functools import partial

import jax
import jax.numpy as jnp
import numpy as np
from jax import lax
from jax.experimental import pallas as pl
from jax.experimental.pallas import tpu as pltpu
from jax.sharding import PartitionSpec as P

H = 16
HD = 64
LAYERS = 2
PAIRS = H // 2
EDGE = 32
LANES = 256
NORM_EPSILON = 1e-05
MASKED_SCORE = -1000000000.0
SCORE_SCALE = 0.125
F32 = jnp.float32
BF16 = jnp.bfloat16
MIB = 1 << 20


def nn(a, b):
    return lax.dot_general(a, b, (((1,), (0,)), ((), ())), preferred_element_type=F32)


def nt(a, b):
    return lax.dot_general(a, b, (((1,), (1,)), ((), ())), preferred_element_type=F32)


def ds(start, size):
    return pl.ds(pl.multiple_of(start, size), size)


def layer_norm(hidden, gain, shift):
    centered = hidden - jnp.mean(hidden, -1, keepdims=True)
    inverse = lax.rsqrt(jnp.mean(centered * centered, -1, keepdims=True) + NORM_EPSILON)
    normed = centered * inverse
    return normed * gain + shift, normed, inverse


def norm_back(grad_out, gain, normed, inverse):
    scaled = grad_out * gain
    return inverse * (
        scaled
        - jnp.mean(scaled, -1, keepdims=True)
        - normed * jnp.mean(scaled * normed, -1, keepdims=True)
    )


def start_loads(tables, pieces, weights, sems):
    width = weights.shape[1]
    for piece, entries in zip(pieces, tables):
        rows = piece.shape[1]

        def start(i, carry, piece=piece, entries=entries, rows=rows):
            row = entries[2 * i + 1]
            pltpu.make_async_copy(piece.at[entries[2 * i]], weights.at[ds(row, rows)], sems.at[row // width]).start()
            return carry

        lax.fori_loop(0, entries.shape[0] // 2, start, 0)


def wait_load(weights, sems, index):
    width = weights.shape[1]
    part = weights.at[pl.ds(index * width, width)]
    pltpu.make_async_copy(part, part, sems.at[index]).wait()


def pair_blocks(half):
    zero = jnp.zeros((HD, LANES), half.dtype)
    return jnp.concatenate(
        [
            jnp.concatenate([half[:HD], zero], 1),
            jnp.concatenate([zero, half[HD:]], 1),
        ],
        0,
    )


def attention_kernel(count, *refs):
    tables, pieces, refs = refs[:count], refs[count : 2 * count], refs[2 * count :]
    (own, near, across, edge, residual, bias, prefix_k, prefix_v, gain, shift) = refs[:10]
    (middle, normed, inverse, query_t, value8, key_t, attend, heads_t) = refs[10:18]
    (weights, window, key8, value_t, scores, sems) = refs[18:]
    tokens, width = own.shape
    span = window.shape[0]
    keys = key8.shape[1]
    start_loads(tables, pieces, weights, sems)
    window[pl.ds(0, tokens)] = own[...]
    window[pl.ds(tokens, tokens)] = near[...]
    window[pl.ds(2 * tokens, tokens)] = across[...]
    window[pl.ds(3 * tokens, EDGE)] = edge[...]
    pad = jnp.zeros((LANES - tokens, 256), BF16)
    for index in range(3):
        wait_load(weights, sems, index)

    def tile(j, carry):
        columns = ds(j * 256, 256)
        query = (SCORE_SCALE * nn(own[...], weights[pl.ds(0, width), columns])).astype(BF16)
        query_t[columns, :] = jnp.concatenate([query, pad], 0).T
        for row, prefix, split, turned in ((width, prefix_k, key8, key_t), (2 * width, prefix_v, value8, value_t)):
            local = nn(window[...], weights[pl.ds(row, width), columns]).astype(BF16)
            whole = jnp.concatenate([local, prefix[:, columns]], 0)
            split[2 * j] = whole[:, :128]
            split[2 * j + 1] = whole[:, 128:]
            turned[columns, :] = whole.T
        return carry

    lax.fori_loop(0, width // 256, tile, 0)
    wide = jnp.zeros((1, 2 * LANES), F32)
    step = 128

    def pair(p, carry):
        blocks = pair_blocks(query_t[ds(p * 128, 128), :])
        top = wide + 2 * MASKED_SCORE
        for c in range(0, keys, step):
            part = nn(key8[p, pl.ds(c, step), :], blocks)
            mask = bias[pl.ds(c, step), :]
            part = part + jnp.concatenate([mask, mask], 1)
            scores[pl.ds(c, step), :] = part
            top = jnp.maximum(top, jnp.max(part, 0, keepdims=True))
        total = wide
        for c in range(0, keys, step):
            part = jnp.exp(scores[pl.ds(c, step), :] - top)
            scores[pl.ds(c, step), :] = part
            total = total + jnp.sum(part, 0, keepdims=True)
        scale = 1.0 / total
        for c in range(0, keys, step):
            attend[p, pl.ds(c, step), :] = (scores[pl.ds(c, step), :] * scale).astype(BF16)
        for half in range(2):
            rows = pl.ds(pl.multiple_of(p * 128 + half * HD, HD), HD)
            heads_t[rows, :] = nn(value_t[rows, :], attend[p, :, pl.ds(half * LANES, LANES)])
        return carry

    lax.fori_loop(0, PAIRS, pair, 0)
    wait_load(weights, sems, 3)
    heads = heads_t[...].astype(BF16).T[:tokens]

    def out(j, carry):
        columns = ds(j * 256, 256)
        middle[:, columns] = residual[:, columns] + nn(heads, weights[pl.ds(3 * width, width), columns])
        return carry

    lax.fori_loop(0, width // 256, out, 0)
    result, n, r = layer_norm(middle[...], gain[...], shift[...])
    middle[...] = result
    normed[...] = n
    inverse[...] = r


def forward_kernel(count, *refs):
    tables, pieces, refs = refs[:count], refs[count : 2 * count], refs[2 * count :]
    (middle, up_bias, gain, shift) = refs[:4]
    (output, low, normed, inverse, slope) = refs[4:9]
    (weights, middle_low, hidden, sems) = refs[9:]
    tokens, width = middle.shape
    wide = up_bias.shape[1]
    start_loads(tables, pieces, weights, sems)
    middle_low[...] = middle[...].astype(BF16)
    for block in range(wide // width):
        wait_load(weights, sems, block)

        def tile(j, carry, block=block):
            columns = ds(j * 256, 256)
            place = ds(block * width + j * 256, 256)
            u = nn(middle_low[...], weights[pl.ds(block * width, width), columns]) + up_bias[:, place]
            part = 0.5 + 0.5 * lax.erf(u * (0.5**0.5))
            hidden[:, place] = (u * part).astype(BF16)
            slope[:, place] = (part + u * (jnp.exp(-0.5 * u * u) * ((2 * np.pi) ** -0.5))).astype(BF16)
            return carry

        lax.fori_loop(0, width // 256, tile, 0)
    for block in range(wide // width):
        wait_load(weights, sems, wide // width + block)

    def down(j, carry):
        columns = ds(j * 256, 256)
        output[:, columns] = middle[:, columns] + nn(hidden[...], weights[pl.ds(wide, wide), columns])
        return carry

    lax.fori_loop(0, width // 256, down, 0)
    result, n, r = layer_norm(output[...], gain[...], shift[...])
    output[...] = result
    low[...] = result.astype(BF16)
    normed[...] = n
    inverse[...] = r


def forward_back_kernel(count, *refs):
    tables, pieces, refs = refs[:count], refs[count : 2 * count], refs[2 * count :]
    (grad, normed_two, inverse_two, gain_two, slope, normed_one, inverse_one, gain_one) = refs[:8]
    (grad_one, heads_grad) = refs[8:10]
    (weights, low, hidden, sems) = refs[10:]
    tokens, width = grad.shape
    wide = slope.shape[1]
    many = wide // width
    start_loads(tables, pieces, weights, sems)
    grad_two = norm_back(grad[...], gain_two[...], normed_two[...], inverse_two[...])
    grad_one[...] = grad_two
    low[pl.ds(0, tokens), :] = grad_two.astype(BF16)
    low[pl.ds(tokens, LANES - tokens), :] = jnp.zeros((LANES - tokens, width), BF16)
    for block in range(many):
        wait_load(weights, sems, many + block)

        def tile(j, carry, block=block):
            place = ds(block * width + j * 256, 256)
            back = nt(low[pl.ds(0, tokens), :], weights[pl.ds(pl.multiple_of(wide + block * width + j * 256, 256), 256), :])
            hidden[:, place] = (back * slope[:, place].astype(F32)).astype(BF16)
            return carry

        lax.fori_loop(0, width // 256, tile, 0)
    for block in range(many):
        wait_load(weights, sems, block)

    def up(j, carry):
        columns = ds(j * 256, 256)
        total = grad_one[:, columns]
        for block in range(many):
            rows = pl.ds(pl.multiple_of(block * width + j * 256, 256), 256)
            total = total + nt(hidden[:, pl.ds(block * width, width)], weights[rows, :])
        grad_one[:, columns] = total
        return carry

    lax.fori_loop(0, width // 256, up, 0)
    back = norm_back(grad_one[...], gain_one[...], normed_one[...], inverse_one[...])
    grad_one[...] = back
    low[pl.ds(0, tokens), :] = back.astype(BF16)
    wait_load(weights, sems, 2 * many)

    def out(j, carry):
        rows = ds(j * 256, 256)
        place = pl.ds(pl.multiple_of(2 * wide + j * 256, 256), 256)
        heads_grad[rows, :] = nt(weights[place, :], low[...]).astype(BF16)
        return carry

    lax.fori_loop(0, width // 256, out, 0)


def attention_back_kernel(count, *refs):
    tables, pieces, refs = refs[:count], refs[count : 2 * count], refs[2 * count :]
    (heads_grad, heads_t, query_t, value8, key_t, attend_hbm) = refs[:6]
    (query_grad, key_own, value_own, halo, prefix_grad) = refs[6:11]
    (weights, attend, key_grad, value_grad, query_grad_t, steps, sems, attend_sems) = refs[11:]
    tokens, width = query_grad.shape
    keys = attend.shape[1]
    prefix = prefix_grad.shape[1]
    span = keys - prefix
    for p in range(PAIRS):
        pltpu.make_async_copy(attend_hbm.at[p], attend.at[p], attend_sems.at[p]).start()
    start_loads(tables, pieces, weights, sems)
    step = 128

    def pair(p, carry):
        pltpu.make_async_copy(attend_hbm.at[p], attend.at[p], attend_sems.at[p]).wait()
        rows = ds(p * 128, 128)
        grad_t = heads_grad[rows, :]
        product = grad_t.astype(F32) * heads_t[rows, :]
        dots = jnp.concatenate(
            [jnp.sum(product[:HD], 0, keepdims=True), jnp.sum(product[HD:], 0, keepdims=True)], 1
        )
        blocks = pair_blocks(grad_t)
        for c in range(0, keys, step):
            part = nn(value8[p, pl.ds(c, step), :], blocks) - dots
            steps[pl.ds(c, step), :] = (attend[p, pl.ds(c, step), :].astype(F32) * part).astype(BF16)
        columns = ds(p * 128, 128)
        grad_v = nt(attend[p], blocks)
        value_grad[:, columns] = grad_v.astype(BF16)
        prefix_grad[1, :, columns] = grad_v[span:]
        grad_k = nt(steps[...], pair_blocks(query_t[rows, :]))
        key_grad[:, columns] = grad_k.astype(BF16)
        prefix_grad[0, :, columns] = grad_k[span:]
        for half in range(2):
            place = pl.ds(pl.multiple_of(p * 128 + half * HD, HD), HD)
            query_grad_t[place, :] = nn(key_t[place, :], steps[:, pl.ds(half * LANES, LANES)]).astype(BF16)
        return carry

    lax.fori_loop(0, PAIRS, pair, 0)
    query_grad[...] = query_grad_t[...].T[:tokens]
    key_own[...] = key_grad[pl.ds(0, tokens), :]
    value_own[...] = value_grad[pl.ds(0, tokens), :]
    wait_load(weights, sems, 0)
    wait_load(weights, sems, 1)

    def outer(j, carry):
        columns = ds(j * 256, 256)
        place = pl.ds(pl.multiple_of(width + j * 256, 256), 256)
        halo[:, columns] = (
            nt(key_grad[pl.ds(tokens, span - tokens), :], weights[columns, :])
            + nt(value_grad[pl.ds(tokens, span - tokens), :], weights[place, :])
        ).astype(BF16)
        return carry

    lax.fori_loop(0, width // 256, outer, 0)


def input_back_kernel(count, *refs):
    tables, pieces, refs = refs[:count], refs[count : 2 * count], refs[2 * count :]
    (grad_one, query_grad, key_own, value_own) = refs[:4]
    grad_input = refs[4]
    (weights, sems) = refs[5:]
    width = grad_one.shape[1]
    start_loads(tables, pieces, weights, sems)
    for index in range(3):
        wait_load(weights, sems, index)

    def tile(j, carry):
        columns = ds(j * 256, 256)
        rows = [pl.ds(pl.multiple_of(i * width + j * 256, 256), 256) for i in range(3)]
        grad_input[:, columns] = (
            grad_one[:, columns]
            + SCORE_SCALE * nt(query_grad[...], weights[rows[0], :])
            + nt(key_own[...], weights[rows[1], :])
            + nt(value_own[...], weights[rows[2], :])
        )
        return carry

    lax.fori_loop(0, width // 256, tile, 0)


VMEM = pl.BlockSpec(memory_space=pltpu.VMEM)
SMEM = pl.BlockSpec(memory_space=pltpu.SMEM)
ANY = pl.BlockSpec(memory_space=pl.ANY)


def call(kernel, weights, operands, kept, outs, scratch, limit, flops):
    tables, pieces = weights
    moved = sum(x.size * x.dtype.itemsize for x in operands)
    moved += sum(len(t) * p[0].size * p.dtype.itemsize for t, p in zip(tables, pieces))
    tables = [jnp.asarray(np.asarray(x).reshape(-1), jnp.int32) for x in tables]
    return pl.pallas_call(
        partial(kernel, len(pieces)),
        out_shape=outs,
        in_specs=[SMEM] * len(tables) + [ANY] * len(pieces) + [VMEM] * len(operands) + [ANY] * len(kept),
        out_specs=[VMEM] * len(outs),
        scratch_shapes=scratch,
        compiler_params=pltpu.CompilerParams(vmem_limit_bytes=limit * MIB),
        cost_estimate=pl.CostEstimate(flops=flops, bytes_accessed=moved, transcendentals=0),
    )(*tables, *pieces, *operands, *kept)


def shape(*sizes, dtype=BF16):
    return jax.ShapeDtypeStruct(sizes, dtype)


def attention_forward(inputs, inputs_low, around, bias, prefix_k, prefix_v, gain, shift, weights):
    tokens, width = inputs.shape
    keys = bias.shape[0]
    span = keys - prefix_k.shape[0]
    return call(
        attention_kernel,
        weights,
        [inputs_low, *around, inputs, bias, prefix_k, prefix_v, gain, shift],
        [],
        [
            shape(tokens, width, dtype=F32),
            shape(tokens, width, dtype=F32),
            shape(tokens, 1, dtype=F32),
            shape(width, LANES),
            shape(PAIRS, keys, 128),
            shape(width, keys),
            shape(PAIRS, keys, 2 * LANES),
            shape(width, LANES, dtype=F32),
        ],
        [
            pltpu.VMEM((4 * width, width), BF16),
            pltpu.VMEM((span, width), BF16),
            pltpu.VMEM((PAIRS, keys, 128), BF16),
            pltpu.VMEM((width, keys), BF16),
            pltpu.VMEM((keys, 2 * LANES), F32),
            pltpu.SemaphoreType.DMA((4,)),
        ],
        40,
        2 * tokens * width * width * 8,
    )


def feed_forward(middle, up_bias, gain, shift, weights):
    tokens, width = middle.shape
    wide = up_bias.shape[1]
    many = wide // width
    return call(
        forward_kernel,
        weights,
        [middle, up_bias, gain, shift],
        [],
        [
            shape(tokens, width, dtype=F32),
            shape(tokens, width),
            shape(tokens, width, dtype=F32),
            shape(tokens, 1, dtype=F32),
            shape(tokens, wide),
        ],
        [
            pltpu.VMEM((2 * wide, width), BF16),
            pltpu.VMEM((tokens, width), BF16),
            pltpu.VMEM((tokens, wide), BF16),
            pltpu.SemaphoreType.DMA((2 * many,)),
        ],
        40,
        4 * tokens * width * wide,
    )


def feed_back(grad, saved_two, gain_two, slope, saved_one, gain_one, weights):
    tokens, width = grad.shape
    wide = slope.shape[1]
    many = wide // width
    return call(
        forward_back_kernel,
        weights,
        [grad, *saved_two, gain_two, slope, *saved_one, gain_one],
        [],
        [shape(tokens, width, dtype=F32), shape(width, LANES)],
        [
            pltpu.VMEM((2 * wide + width, width), BF16),
            pltpu.VMEM((LANES, width), BF16),
            pltpu.VMEM((tokens, wide), BF16),
            pltpu.SemaphoreType.DMA((2 * many + 1,)),
        ],
        40,
        4 * tokens * width * wide + 2 * tokens * width * width,
    )


def attention_back(heads_grad, heads_t, query_t, value8, key_t, attend, tokens, prefix, weights):
    width = heads_grad.shape[0]
    keys = attend.shape[1]
    span = keys - prefix
    return call(
        attention_back_kernel,
        weights,
        [heads_grad, heads_t, query_t, value8, key_t],
        [attend],
        [
            shape(tokens, width),
            shape(tokens, width),
            shape(tokens, width),
            shape(span - tokens, width),
            shape(2, prefix, width, dtype=F32),
        ],
        [
            pltpu.VMEM((2 * width, width), BF16),
            pltpu.VMEM(attend.shape, BF16),
            pltpu.VMEM((keys, width), BF16),
            pltpu.VMEM((keys, width), BF16),
            pltpu.VMEM((width, LANES), BF16),
            pltpu.VMEM((keys, 2 * LANES), BF16),
            pltpu.SemaphoreType.DMA((2,)),
            pltpu.SemaphoreType.DMA((PAIRS,)),
        ],
        40,
        2 * tokens * width * keys * 8,
    )


def input_back(grad_one, query_grad, key_own, value_own, weights):
    tokens, width = grad_one.shape
    return call(
        input_back_kernel,
        weights,
        [grad_one, query_grad, key_own, value_own],
        [],
        [shape(tokens, width, dtype=F32)],
        [pltpu.VMEM((3 * width, width), BF16), pltpu.SemaphoreType.DMA((3,))],
        30,
        6 * tokens * width * width,
    )[0]


def xor_pairs(count, bit):
    return [(i, i ^ bit) for i in range(count)]


def sum_prefixes(parts):
    layers, two, prefix, width = parts.shape
    places = lax.axis_size("keys")
    place = lax.axis_index("keys")
    total = parts
    step = places // 2
    while step:
        split = total.reshape(layers, two, 2, -1, width)
        mine = (place // step) % 2
        sent = lax.dynamic_index_in_dim(split, 1 - mine, 2, False).astype(BF16)
        kept = lax.dynamic_index_in_dim(split, mine, 2, False)
        total = kept + lax.ppermute(sent, "keys", xor_pairs(places, step)).astype(F32)
        step //= 2
    count = lax.axis_size("rows")
    step = 1
    while step < count:
        total = total + lax.ppermute(total.astype(BF16), "rows", xor_pairs(count, step)).astype(F32)
        step *= 2
    return total


def body(
    activations,
    segments,
    prefix_keys,
    prefix_values,
    w_query,
    w_key,
    w_value,
    w_out,
    w_up,
    ff_bias,
    w_down,
    ln_gain,
    ln_bias,
    cotangent,
):
    _, tokens, width = activations.shape
    wide = w_up.shape[2]
    ratio = wide // width
    places = lax.axis_size("keys")
    parts = lax.axis_size("rows")
    rows = width // parts
    place = lax.axis_index("keys")
    prefix = prefix_keys.shape[1] * places
    first_half = place < places // 2

    def attention_blocks(layer):
        return jnp.stack([w_query[layer], w_key[layer], w_value[layer], w_out[layer]])

    def feed_blocks(layer):
        up = [w_up[layer][:, i * width : (i + 1) * width] for i in range(ratio)]
        down = [w_down[layer][i * rows : (i + 1) * rows] for i in range(ratio)]
        return jnp.stack(up + down)

    def share_of(blocks):
        count = blocks.shape[0] // places
        return lax.dynamic_slice_in_dim(blocks, place * count, count, 0)

    def gather(*shares):
        return lax.all_gather(jnp.concatenate(shares, 0), ("rows", "keys"), axis=0, tiled=True)

    first = gather(share_of(attention_blocks(0)), share_of(feed_blocks(0)), share_of(attention_blocks(1)))
    second = gather(share_of(feed_blocks(1)))
    each = 2 * ratio // places
    many = each + 2

    def attention_table(start, size, kinds):
        return [
            ((r * places + kind) * size + start, i * width + r * rows)
            for i, kind in enumerate(kinds)
            for r in range(parts)
        ]

    def feed_table(start, size):
        return [
            (
                (r * places + b // each) * size + start + b % each,
                b * width + r * rows if b < ratio else wide + (r * ratio + b - ratio) * rows,
            )
            for b in range(2 * ratio)
            for r in range(parts)
        ]

    attention_places = [(first, 0, many), (first, many - 1, many)]
    feed_places = [(first, 1, many), (second, 0, each)]

    def attention_weights(layer, *kinds):
        gathered, start, size = attention_places[layer]
        return [attention_table(start, size, kinds)], [gathered]

    def feed_weights(layer):
        gathered, start, size = feed_places[layer]
        return [feed_table(start, size)], [gathered]

    def joined(left, right, offset):
        moved = [[(i, row + offset) for i, row in table] for table in right[0]]
        return left[0] + moved, left[1] + right[1]

    def exchange(low):
        near = lax.ppermute(low, "keys", xor_pairs(places, 1))
        across = lax.ppermute(low, "keys", [(1, 2), (2, 1)])
        edge = lax.ppermute(
            jnp.where(first_half, low[tokens - EDGE :], low[:EDGE]), "keys", xor_pairs(places, 2)
        )
        return near, across, edge

    line = segments[0]

    def ids(where, start, size):
        return lax.dynamic_slice_in_dim(line, where * tokens + start, size, 0)

    own_ids = ids(place, 0, tokens)
    across_ids = jnp.where(
        (place == 1) | (place == 2), ids(jnp.clip(3 - place, 0, places - 1), 0, tokens), -1
    )
    edge_ids = ids(place ^ 2, jnp.where(first_half, 0, tokens - EDGE), EDGE)
    key_ids = jnp.concatenate([own_ids, ids(place ^ 1, 0, tokens), across_ids, edge_ids])
    allowed = jnp.concatenate([key_ids[:, None] == own_ids[None, :], jnp.ones((prefix, tokens), bool)], 0)
    bias = jnp.pad(jnp.where(allowed, 0.0, MASKED_SCORE).astype(F32), ((0, 0), (0, LANES - tokens)))

    prefixes = lax.all_gather(jnp.stack([prefix_keys, prefix_values]), "keys", axis=2, tiled=True)

    low = activations[0]
    hidden = low.astype(F32)
    saved = []
    for layer in range(LAYERS):
        gains, shifts = ln_gain[layer][:, None], ln_bias[layer][:, None]
        around = exchange(low)
        middle, normed_one, inverse_one, query_t, value8, key_t, attend, heads_t = attention_forward(
            hidden,
            low,
            around,
            bias,
            prefixes[0, layer],
            prefixes[1, layer],
            gains[0],
            shifts[0],
            attention_weights(layer, 0, 1, 2, 3),
        )
        hidden, low, normed_two, inverse_two, slope = feed_forward(
            middle, ff_bias[layer][None], gains[1], shifts[1], feed_weights(layer)
        )
        saved.append(
            ((normed_one, inverse_one), (normed_two, inverse_two), slope, heads_t, query_t, value8, key_t, attend)
        )
    result = low

    gradient = cotangent[0].astype(F32)
    prefix_parts = [None] * LAYERS
    for layer in range(LAYERS - 1, -1, -1):
        saved_one, saved_two, slope, heads_t, query_t, value8, key_t, attend = saved[layer]
        gains = ln_gain[layer][:, None]
        grad_one, heads_grad = feed_back(
            gradient,
            saved_two,
            gains[1],
            slope,
            saved_one,
            gains[0],
            joined(feed_weights(layer), attention_weights(layer, 3), 2 * wide),
        )
        query_grad, key_own, value_own, halo, prefix_grad = attention_back(
            heads_grad, heads_t, query_t, value8, key_t, attend, tokens, prefix, attention_weights(layer, 1, 2)
        )
        near = lax.ppermute(halo[:tokens], "keys", xor_pairs(places, 1))
        across = lax.ppermute(halo[tokens : 2 * tokens], "keys", [(1, 2), (2, 1)])
        edge = lax.ppermute(halo[2 * tokens :], "keys", xor_pairs(places, 2)).astype(F32)
        gradient = input_back(grad_one, query_grad, key_own, value_own, attention_weights(layer, 0, 1, 2))
        lead = jnp.where(first_half, 0.0, edge)
        tail = jnp.where(first_half, edge, 0.0)
        gradient = (
            gradient
            + near.astype(F32)
            + across.astype(F32)
            + jnp.concatenate([lead, jnp.zeros((tokens - 2 * EDGE, width), F32), tail], 0)
        )
        prefix_parts[layer] = prefix_grad
    prefix_total = sum_prefixes(jnp.stack(prefix_parts))
    return (
        result[None],
        gradient[None],
        prefix_total[:, 0],
        prefix_total[:, 1],
    )


def solution(mesh):
    placed = (
        P("rows", "keys", None),
        P("rows", None),
        P(None, "keys", None),
        P(None, "keys", None),
        P(None, "rows", None),
        P(None, "rows", None),
        P(None, "rows", None),
        P(None, "rows", None),
        P(None, "rows", None),
        P(),
        P(None, "rows", None),
        P(),
        P(),
        P("rows", "keys", None),
    )
    return jax.shard_map(
        body,
        mesh=mesh,
        in_specs=placed,
        out_specs=(
            P("rows", "keys", None),
            P("rows", "keys", None),
            P(None, "keys", None),
            P(None, "keys", None),
        ),
        check_vma=False,
    )
```

```python
from functools import partial

import jax
import jax.numpy as jnp
import numpy as np
from jax import lax
from jax.experimental import pallas as pl
from jax.experimental.pallas import tpu as pltpu
from jax.sharding import PartitionSpec as P

H = 16
HD = 64
LAYERS = 2
PAIRS = H // 2
EDGE = 32
LANES = 256
NORM_EPSILON = 1e-05
MASKED_SCORE = -1000000000.0
SCORE_SCALE = 0.125
F32 = jnp.float32
BF16 = jnp.bfloat16
MIB = 1 << 20


def nn(a, b):
    return lax.dot_general(a, b, (((1,), (0,)), ((), ())), preferred_element_type=F32)


def nt(a, b):
    return lax.dot_general(a, b, (((1,), (1,)), ((), ())), preferred_element_type=F32)


def ds(start, size):
    return pl.ds(pl.multiple_of(start, size), size)


def layer_norm(hidden, gain, shift):
    centered = hidden - jnp.mean(hidden, -1, keepdims=True)
    inverse = lax.rsqrt(jnp.mean(centered * centered, -1, keepdims=True) + NORM_EPSILON)
    normed = centered * inverse
    return normed * gain + shift, normed, inverse


def norm_back(grad_out, gain, normed, inverse):
    scaled = grad_out * gain
    return inverse * (
        scaled
        - jnp.mean(scaled, -1, keepdims=True)
        - normed * jnp.mean(scaled * normed, -1, keepdims=True)
    )


class Loads:
    def __init__(self, sems):
        self.sems, self.copies, self.count = sems, {}, 0

    def start(self, name, source, target):
        copy = pltpu.make_async_copy(source, target, self.sems.at[self.count])
        copy.start()
        self.copies[name] = copy
        self.count += 1

    def wait(self, *names):
        for name in names:
            copy = self.copies.pop(name, None)
            if copy is not None:
                copy.wait()


def square(ref, columns=slice(None)):
    block = ref[:, :, columns]
    return block.reshape(block.shape[0] * block.shape[1], block.shape[2])


def load_attention(loads, gathered, start, kinds, weights):
    for i, kind in enumerate(kinds):
        loads.start(("square", kind), gathered.at[:, kind, start], weights.at[i])


def load_up(loads, gathered, start, up):
    each = up.shape[0] // (gathered.shape[1] // 2)
    for b in range(up.shape[0]):
        loads.start(("up", b), gathered.at[:, b // each, start + b % each], up.at[b])


def load_down(loads, gathered, start, down):
    half, each = down.shape[1:3]
    for r in range(down.shape[0]):
        loads.start(("down", r), gathered.at[r, pl.ds(half, half), pl.ds(start, each)], down.at[r])


def pair_blocks(half):
    zero = jnp.zeros((HD, LANES), half.dtype)
    return jnp.concatenate(
        [
            jnp.concatenate([half[:HD], zero], 1),
            jnp.concatenate([zero, half[HD:]], 1),
        ],
        0,
    )


def attention_kernel(start, *refs):
    (gathered, own, near, across, edge, residual, bias, prefix_k, prefix_v, gain, shift) = refs[:11]
    (middle, normed, inverse, query_t, value8, key_t, attend, heads_t) = refs[11:19]
    (weights, window, key8, value_t, scores, sems) = refs[19:]
    tokens, width = own.shape
    keys = key8.shape[1]
    loads = Loads(sems)
    load_attention(loads, gathered, start, range(4), weights)
    window[pl.ds(0, tokens)] = own[...]
    window[pl.ds(tokens, tokens)] = near[...]
    window[pl.ds(2 * tokens, tokens)] = across[...]
    window[pl.ds(3 * tokens, EDGE)] = edge[...]
    pad = jnp.zeros((LANES - tokens, 256), BF16)
    for kind in range(3):
        loads.wait(("square", kind))

    def tile(j, carry):
        columns = ds(j * 256, 256)
        query = (SCORE_SCALE * nn(own[...], square(weights.at[0], columns))).astype(BF16)
        query_t[columns, :] = jnp.concatenate([query, pad], 0).T
        for kind, prefix, split, turned in ((1, prefix_k, key8, key_t), (2, prefix_v, value8, value_t)):
            local = nn(window[...], square(weights.at[kind], columns)).astype(BF16)
            whole = jnp.concatenate([local, prefix[:, columns]], 0)
            split[2 * j] = whole[:, :128]
            split[2 * j + 1] = whole[:, 128:]
            turned[columns, :] = whole.T
        return carry

    lax.fori_loop(0, width // 256, tile, 0, unroll=2)
    wide = jnp.zeros((1, 2 * LANES), F32)
    step = 128

    def pair(p, carry):
        blocks = pair_blocks(query_t[ds(p * 128, 128), :])
        top = wide + 2 * MASKED_SCORE
        for c in range(0, keys, step):
            part = nn(key8[p, pl.ds(c, step), :], blocks)
            mask = bias[pl.ds(c, step), :]
            part = part + jnp.concatenate([mask, mask], 1)
            scores[pl.ds(c, step), :] = part
            top = jnp.maximum(top, jnp.max(part, 0, keepdims=True))
        total = wide
        for c in range(0, keys, step):
            part = jnp.exp(scores[pl.ds(c, step), :] - top)
            scores[pl.ds(c, step), :] = part
            total = total + jnp.sum(part, 0, keepdims=True)
        scale = 1.0 / total
        for c in range(0, keys, step):
            attend[p, pl.ds(c, step), :] = (scores[pl.ds(c, step), :] * scale).astype(BF16)
        for half in range(2):
            rows = pl.ds(pl.multiple_of(p * 128 + half * HD, HD), HD)
            heads_t[rows, :] = nn(value_t[rows, :], attend[p, :, pl.ds(half * LANES, LANES)])
        return carry

    lax.fori_loop(0, PAIRS, pair, 0)
    loads.wait(("square", 3))
    heads = heads_t[...].astype(BF16).T[:tokens]
    for c in range(0, width, 512):
        columns = pl.ds(c, 512)
        middle[:, columns] = residual[:, columns] + nn(heads, square(weights.at[3], columns))
    result, n, r = layer_norm(middle[...], gain[...], shift[...])
    middle[...] = result
    normed[...] = n
    inverse[...] = r


def feed_forward_steps(loads, middle, up_bias, gain, shift, up, down, low, hidden, slope, output):
    tokens, width = middle.shape
    low[pl.ds(0, tokens), :] = middle[...].astype(BF16)
    for b in range(up.shape[0]):
        loads.wait(("up", b))
        for c in range(0, width, 512):
            place = pl.ds(b * width + c, 512)
            u = nn(low[pl.ds(0, tokens), :], square(up.at[b], pl.ds(c, 512))) + up_bias[:, place]
            part = 0.5 + 0.5 * lax.erf(u * (0.5**0.5))
            hidden[:, place] = (u * part).astype(BF16)
            slope[:, place] = (part + u * (jnp.exp(-0.5 * u * u) * ((2 * np.pi) ** -0.5))).astype(BF16)
    for r in range(down.shape[0]):
        loads.wait(("down", r))
    for c in range(0, width, 512):
        columns = pl.ds(c, 512)
        block = down[:, :, :, :, columns].reshape(hidden.shape[1], 512)
        output[:, columns] = middle[:, columns] + nn(hidden[...], block)
    return layer_norm(output[...], gain[...], shift[...])


def forward_kernel(start, *refs):
    (gathered, middle, up_bias, gain, shift) = refs[:5]
    (output, low, normed, inverse, slope) = refs[5:10]
    (up, down, hidden, sems) = refs[10:]
    loads = Loads(sems)
    load_up(loads, gathered, start, up)
    load_down(loads, gathered, start, down)
    result, n, r = feed_forward_steps(loads, middle, up_bias, gain, shift, up, down, low, hidden, slope, output)
    output[...] = result
    low[...] = result.astype(BF16)
    normed[...] = n
    inverse[...] = r


def feed_back_steps(loads, grad_two, slope, normed_one, inverse_one, gain_one, up, down, weights, low, hidden, grad_one, heads_grad):
    tokens, width = grad_two.shape
    low[pl.ds(0, tokens), :] = grad_two.astype(BF16)
    grad_one[...] = grad_two
    size = hidden.shape[1] // down.shape[0]
    for r in range(down.shape[0]):
        loads.wait(("down", r))
        place = pl.ds(r * size, size)
        back = nt(low[pl.ds(0, tokens), :], down[r].reshape(size, width))
        hidden[:, place] = (back * slope[:, place].astype(F32)).astype(BF16)
    for b in range(up.shape[0]):
        loads.wait(("up", b))
    rows = up.shape[2]
    for c in range(0, width, 512):
        total = grad_one[:, pl.ds(c, 512)]
        for b in range(up.shape[0]):
            block = up[b, pl.ds(c // rows, 512 // rows)].reshape(512, width)
            total = total + nt(hidden[:, pl.ds(b * width, width)], block)
        grad_one[:, pl.ds(c, 512)] = total
    loads.wait("normed_one")
    back = norm_back(grad_one[...], gain_one[...], normed_one[...], inverse_one[...])
    grad_one[...] = back
    low[pl.ds(0, tokens), :] = back.astype(BF16)
    low[pl.ds(tokens, LANES - tokens), :] = jnp.zeros((LANES - tokens, width), BF16)
    loads.wait(("square", 3))
    heads_grad[...] = nt(square(weights.at[0]), low[...]).astype(BF16)


def attention_back_steps(loads, heads_grad, heads_t, query_t, value8, key_t, attend, weights, key_grad, value_grad, query_grad_t, steps, outs):
    (query_grad, key_own, value_own, halo, prefix_grad) = outs
    tokens, width = query_grad.shape
    keys = attend.shape[1]
    span = keys - prefix_grad.shape[1]
    loads.wait("heads_t", "query_t", "value8", "key_t")
    step = 128
    for p in range(PAIRS):
        loads.wait(("attend", p))
        rows = pl.ds(p * 128, 128)
        grad_t = heads_grad[rows, :]
        product = grad_t.astype(F32) * heads_t[rows, :]
        dots = jnp.concatenate(
            [jnp.sum(product[:HD], 0, keepdims=True), jnp.sum(product[HD:], 0, keepdims=True)], 1
        )
        blocks = pair_blocks(grad_t)
        grad_v = nt(attend[p], blocks)
        value_grad[:, rows] = grad_v.astype(BF16)
        prefix_grad[1, :, rows] = grad_v[span:]
        here = steps.at[p % 2]
        for c in range(0, keys, step):
            part = nn(value8[p, pl.ds(c, step), :], blocks) - dots
            here[pl.ds(c, step), :] = (attend[p, pl.ds(c, step), :].astype(F32) * part).astype(BF16)
        grad_k = nt(here[...], pair_blocks(query_t[rows, :]))
        key_grad[:, rows] = grad_k.astype(BF16)
        prefix_grad[0, :, rows] = grad_k[span:]
        for half in range(2):
            place = pl.ds(p * 128 + half * HD, HD)
            query_grad_t[place, :] = nn(key_t[place, :], here[:, pl.ds(half * LANES, LANES)]).astype(BF16)
    query_grad[...] = query_grad_t[...].T[:tokens]
    key_own[...] = key_grad[pl.ds(0, tokens), :]
    value_own[...] = value_grad[pl.ds(0, tokens), :]
    loads.wait(("square", 1), ("square", 2))
    outer = pl.ds(tokens, span - tokens)
    rows = weights.shape[2]
    for c in range(0, width, 512):
        part = pl.ds(c // rows, 512 // rows)
        halo[:, pl.ds(c, 512)] = (
            nt(key_grad[outer, :], weights[1, part].reshape(512, width))
            + nt(value_grad[outer, :], weights[2, part].reshape(512, width))
        ).astype(BF16)


def load_saved(loads, gathered, start, saved, weights, buffers):
    load_attention(loads, gathered, start, [3], weights.at[pl.ds(0, 1)])
    for name, source, target in zip(("heads_t", "query_t", "value8", "key_t"), saved, buffers):
        loads.start(name, source, target)
    for p in range(PAIRS):
        loads.start(("attend", p), saved[4].at[p], buffers[4].at[p])
    load_attention(loads, gathered, start, [1, 2], weights.at[pl.ds(1, 2)])


def last_kernel(feed_start, attention_start, *refs):
    (feed, squares, middle, up_bias, gain_two, shift_two, cotangent, inverse_one, gain_one, normed_hbm) = refs[:10]
    saved = refs[10:15]
    low_out, grad_one = refs[15:17]
    outs = refs[17:22]
    (up, down, weights, slope, low, hidden, normed_one, heads_grad) = refs[22:30]
    buffers = refs[30:35]
    (key_grad, value_grad, query_grad_t, steps, sems) = refs[35:]
    loads = Loads(sems)
    load_up(loads, feed, feed_start, up)
    load_down(loads, feed, feed_start, down)
    loads.start("normed_one", normed_hbm, normed_one)
    load_saved(loads, squares, attention_start, saved, weights, buffers)
    result, n, r = feed_forward_steps(
        loads, middle, up_bias, gain_two, shift_two, up, down, low, hidden, slope, grad_one
    )
    low_out[...] = result.astype(BF16)
    grad_two = norm_back(cotangent[...].astype(F32), gain_two[...], n, r)
    feed_back_steps(
        loads, grad_two, slope, normed_one, inverse_one, gain_one, up, down, weights, low, hidden, grad_one, heads_grad
    )
    attention_back_steps(
        loads, heads_grad, *buffers[:5], weights, key_grad, value_grad, query_grad_t, steps, outs
    )


def back_kernel(feed_start, attention_start, *refs):
    (flag, feed, squares, grad, near, across, edge, inverse_two, gain_two, inverse_one, gain_one) = refs[:11]
    (normed_two_hbm, slope_hbm, normed_one_hbm) = refs[11:14]
    saved = refs[14:19]
    grad_one = refs[19]
    outs = refs[20:25]
    (up, down, weights, slope, low, hidden, normed_two, normed_one, heads_grad) = refs[25:34]
    buffers = refs[34:39]
    (key_grad, value_grad, query_grad_t, steps, sems) = refs[39:]
    tokens, width = grad.shape
    loads = Loads(sems)
    loads.start("normed_two", normed_two_hbm, normed_two)
    loads.start("slope", slope_hbm, slope)
    load_down(loads, feed, feed_start, down)
    load_up(loads, feed, feed_start, up)
    loads.start("normed_one", normed_one_hbm, normed_one)
    load_saved(loads, squares, attention_start, saved, weights, buffers)
    grad_one[...] = grad[...] + near[...].astype(F32) + across[...].astype(F32)
    last = flag[0].astype(F32)
    extra = edge[...].astype(F32)
    head, tail = pl.ds(0, EDGE), pl.ds(tokens - EDGE, EDGE)
    grad_one[head, :] = grad_one[head, :] + extra * (1.0 - last)
    grad_one[tail, :] = grad_one[tail, :] + extra * last
    loads.wait("normed_two")
    grad_two = norm_back(grad_one[...], gain_two[...], normed_two[...], inverse_two[...])
    loads.wait("slope")
    feed_back_steps(
        loads, grad_two, slope, normed_one, inverse_one, gain_one, up, down, weights, low, hidden, grad_one, heads_grad
    )
    attention_back_steps(
        loads, heads_grad, *buffers[:5], weights, key_grad, value_grad, query_grad_t, steps, outs
    )


def input_back_kernel(start, *refs):
    (gathered, grad_one, query_grad, key_own, value_own, grad_input, weights, sems) = refs
    width = grad_one.shape[1]
    rows = weights.shape[2]
    loads = Loads(sems)
    load_attention(loads, gathered, start, range(3), weights)
    for kind in range(3):
        loads.wait(("square", kind))
        left, scale = ((query_grad, SCORE_SCALE), (key_own, None), (value_own, None))[kind]
        before = grad_one if kind == 0 else grad_input
        for c in range(0, width, 512):
            columns = pl.ds(c, 512)
            part = nt(left[...], weights[kind, pl.ds(c // rows, 512 // rows)].reshape(512, width))
            grad_input[:, columns] = before[:, columns] + (part if scale is None else scale * part)


def pack_kernel(place, query, key, value, out, up, down, first, second, sems):
    places = 4
    half = places // 2
    rows = query.shape[1]
    width = query.shape[2]
    each = second.shape[0]
    for k in range(places):

        @pl.when(place[0] == k)
        def _():
            matrix = (query, key, value, out)[k]
            jobs = [(matrix.at[0], first.at[0]), (matrix.at[1], first.at[each + 1])]
            for layer, target, begin in ((0, first, 1), (1, second, 0)):
                for i in range(each):
                    b = k * each + i
                    if k < half:
                        source = up.at[layer, :, pl.ds(b * width, width)]
                    else:
                        source = down.at[layer, pl.ds((b - half * each) * rows, rows)]
                    jobs.append((source, target.at[begin + i]))
            copies = [pltpu.make_async_copy(a, b, sems.at[i]) for i, (a, b) in enumerate(jobs)]
            for copy in copies:
                copy.start()
            for copy in copies:
                copy.wait()


VMEM = pl.BlockSpec(memory_space=pltpu.VMEM)
SMEM = pl.BlockSpec(memory_space=pltpu.SMEM)
ANY = pl.BlockSpec(memory_space=pl.ANY)


def call(kernel, numbers, kept, operands, late, outs, scratch, limit, flops, sem_count, small=()):
    moved = sum(x.size * x.dtype.itemsize for x in (*operands, *late)) + 16 * MIB
    return pl.pallas_call(
        partial(kernel, *numbers),
        out_shape=outs,
        in_specs=[SMEM] * len(small) + [ANY] * len(kept) + [VMEM] * len(operands) + [ANY] * len(late),
        out_specs=[VMEM] * len(outs),
        scratch_shapes=[*scratch, pltpu.SemaphoreType.DMA((sem_count,))],
        compiler_params=pltpu.CompilerParams(vmem_limit_bytes=limit * MIB),
        cost_estimate=pl.CostEstimate(flops=flops, bytes_accessed=moved, transcendentals=0),
    )(*small, *kept, *operands, *late)


def shape(*sizes, dtype=BF16):
    return jax.ShapeDtypeStruct(sizes, dtype)


def feed_scratch(gathered, wide):
    parts, places, _, rows, width = gathered.shape
    ratio = wide // width
    return [
        pltpu.VMEM((ratio, parts, rows, width), BF16),
        pltpu.VMEM((parts, places // 2, 2 * ratio // places, rows, width), BF16),
    ]


def squares_scratch(gathered, count):
    parts, _, _, rows, width = gathered.shape
    return pltpu.VMEM((count, parts, rows, width), BF16)


def attention_forward(inputs, inputs_low, around, bias, prefix_k, prefix_v, gain, shift, weights):
    gathered, start = weights
    tokens, width = inputs.shape
    keys = bias.shape[0]
    span = keys - prefix_k.shape[0]
    return call(
        attention_kernel,
        [start],
        [gathered],
        [inputs_low, *around, inputs, bias, prefix_k, prefix_v, gain, shift],
        [],
        [
            shape(tokens, width, dtype=F32),
            shape(tokens, width, dtype=F32),
            shape(tokens, 1, dtype=F32),
            shape(width, LANES),
            shape(PAIRS, keys, 128),
            shape(width, keys),
            shape(PAIRS, keys, 2 * LANES),
            shape(width, LANES, dtype=F32),
        ],
        [
            squares_scratch(gathered, 4),
            pltpu.VMEM((span, width), BF16),
            pltpu.VMEM((PAIRS, keys, 128), BF16),
            pltpu.VMEM((width, keys), BF16),
            pltpu.VMEM((keys, 2 * LANES), F32),
        ],
        40,
        2 * tokens * width * width * 8,
        4,
    )


def feed_forward(middle, up_bias, gain, shift, weights):
    gathered, start = weights
    tokens, width = middle.shape
    wide = up_bias.shape[1]
    return call(
        forward_kernel,
        [start],
        [gathered],
        [middle, up_bias, gain, shift],
        [],
        [
            shape(tokens, width, dtype=F32),
            shape(tokens, width),
            shape(tokens, width, dtype=F32),
            shape(tokens, 1, dtype=F32),
            shape(tokens, wide),
        ],
        [*feed_scratch(gathered, wide), pltpu.VMEM((tokens, wide), BF16)],
        40,
        4 * tokens * width * wide,
        wide // width + gathered.shape[0],
    )


def back_shapes(tokens, width, keys, prefix):
    span = keys - prefix
    return [
        shape(tokens, width, dtype=F32),
        shape(tokens, width),
        shape(tokens, width),
        shape(tokens, width),
        shape(span - tokens, width),
        shape(2, prefix, width, dtype=F32),
    ]


def saved_scratch(saved):
    heads_t, query_t, value8, key_t, attend = saved
    keys = attend.shape[1]
    width = heads_t.shape[0]
    return [pltpu.VMEM(x.shape, x.dtype) for x in saved] + [
        pltpu.VMEM((keys, width), BF16),
        pltpu.VMEM((keys, width), BF16),
        pltpu.VMEM((width, LANES), BF16),
        pltpu.VMEM((2, keys, 2 * LANES), BF16),
    ]


def layer_call(kernel, small, operands, late, outs, kinds, saved, feed, squares, wide, tokens):
    gathered = feed[0]
    parts, _, _, _, width = gathered.shape
    ratio = wide // width
    return call(
        kernel,
        [feed[1], squares[1]],
        [feed[0], squares[0]],
        operands,
        [*late, *saved],
        outs,
        [
            *feed_scratch(gathered, wide),
            squares_scratch(gathered, 3),
            pltpu.VMEM((tokens, wide), BF16),
            pltpu.VMEM((LANES, width), BF16),
            pltpu.VMEM((tokens, wide), BF16),
            *[pltpu.VMEM((tokens, width), F32)] * kinds,
            pltpu.VMEM((width, LANES), BF16),
            *saved_scratch(saved),
        ],
        52,
        8 * tokens * width * wide,
        ratio + parts + 3 + 4 + PAIRS + 3,
        small,
    )


def input_back(grad_one, query_grad, key_own, value_own, weights):
    gathered, start = weights
    tokens, width = grad_one.shape
    return call(
        input_back_kernel,
        [start],
        [gathered],
        [grad_one, query_grad, key_own, value_own],
        [],
        [shape(tokens, width, dtype=F32)],
        [squares_scratch(gathered, 3)],
        30,
        6 * tokens * width * width,
        3,
    )[0]


def pack(place, w_query, w_key, w_value, w_out, w_up, w_down, each):
    rows, width = w_query.shape[1:]
    return pl.pallas_call(
        pack_kernel,
        out_shape=[shape(each + 2, rows, width), shape(each, rows, width)],
        in_specs=[SMEM] + [ANY] * 6,
        out_specs=[VMEM] * 2,
        scratch_shapes=[pltpu.SemaphoreType.DMA((2 * each + 2,))],
    )(place, w_query, w_key, w_value, w_out, w_up, w_down)


def xor_pairs(count, bit):
    return [(i, i ^ bit) for i in range(count)]


def sum_prefixes(parts):
    layers, two, prefix, width = parts.shape
    places = lax.axis_size("keys")
    place = lax.axis_index("keys")
    total = parts
    step = places // 2
    while step:
        split = total.reshape(layers, two, 2, -1, width)
        mine = (place // step) % 2
        sent = lax.dynamic_index_in_dim(split, 1 - mine, 2, False).astype(BF16)
        kept = lax.dynamic_index_in_dim(split, mine, 2, False)
        total = kept + lax.ppermute(sent, "keys", xor_pairs(places, step)).astype(F32)
        step //= 2
    count = lax.axis_size("rows")
    step = 1
    while step < count:
        total = total + lax.ppermute(total.astype(BF16), "rows", xor_pairs(count, step)).astype(F32)
        step *= 2
    return total


def body(
    activations,
    segments,
    prefix_keys,
    prefix_values,
    w_query,
    w_key,
    w_value,
    w_out,
    w_up,
    ff_bias,
    w_down,
    ln_gain,
    ln_bias,
    cotangent,
):
    _, tokens, width = activations.shape
    wide = w_up.shape[2]
    ratio = wide // width
    places = lax.axis_size("keys")
    parts = lax.axis_size("rows")
    rows = width // parts
    place = lax.axis_index("keys")
    prefix = prefix_keys.shape[1] * places
    first_half = place < places // 2

    each = 2 * ratio // places
    shares = pack(place[None], w_query, w_key, w_value, w_out, w_up, w_down, each)

    def gather(share):
        whole = lax.all_gather(share, ("rows", "keys"), axis=0, tiled=True)
        return whole.reshape(parts, places, share.shape[0], rows, width)

    first, second = gather(shares[0]), gather(shares[1])
    squares = [(first, 0), (first, each + 1)]
    feeds = [(first, 1), (second, 0)]

    def exchange(low):
        near = lax.ppermute(low, "keys", xor_pairs(places, 1))
        across = lax.ppermute(low, "keys", [(1, 2), (2, 1)])
        edge = lax.ppermute(
            jnp.where(first_half, low[tokens - EDGE :], low[:EDGE]), "keys", xor_pairs(places, 2)
        )
        return near, across, edge

    line = segments[0]

    def ids(where, start, size):
        return lax.dynamic_slice_in_dim(line, where * tokens + start, size, 0)

    own_ids = ids(place, 0, tokens)
    across_ids = jnp.where(
        (place == 1) | (place == 2), ids(jnp.clip(3 - place, 0, places - 1), 0, tokens), -1
    )
    edge_ids = ids(place ^ 2, jnp.where(first_half, 0, tokens - EDGE), EDGE)
    key_ids = jnp.concatenate([own_ids, ids(place ^ 1, 0, tokens), across_ids, edge_ids])
    allowed = jnp.concatenate([key_ids[:, None] == own_ids[None, :], jnp.ones((prefix, tokens), bool)], 0)
    bias = jnp.pad(jnp.where(allowed, 0.0, MASKED_SCORE).astype(F32), ((0, 0), (0, LANES - tokens)))

    prefixes = lax.all_gather(jnp.stack([prefix_keys, prefix_values]), "keys", axis=2, tiled=True)

    low = activations[0]
    hidden = low.astype(F32)
    kept, kept_feed = [], []
    for layer in range(LAYERS):
        gains, shifts = ln_gain[layer][:, None], ln_bias[layer][:, None]
        around = exchange(low)
        middle, normed_one, inverse_one, query_t, value8, key_t, attend, heads_t = attention_forward(
            hidden,
            low,
            around,
            bias,
            prefixes[0, layer],
            prefixes[1, layer],
            gains[0],
            shifts[0],
            squares[layer],
        )
        saved = (heads_t, query_t, value8, key_t, attend)
        kept.append(((normed_one, inverse_one), saved))
        if layer < LAYERS - 1:
            hidden, low, *second_norm = feed_forward(middle, ff_bias[layer][None], gains[1], shifts[1], feeds[layer])
            kept_feed.append(second_norm)

    flag = first_half.astype(jnp.int32)[None]
    keys = bias.shape[0]
    prefix_parts = [None] * LAYERS
    for layer in range(LAYERS - 1, -1, -1):
        (normed_one, inverse_one), saved = kept[layer]
        gains, shifts = ln_gain[layer][:, None], ln_bias[layer][:, None]
        outs = back_shapes(tokens, width, keys, prefix)
        if layer == LAYERS - 1:
            result, grad_one, query_grad, key_own, value_own, halo, prefix_parts[layer] = layer_call(
                last_kernel,
                (),
                [middle, ff_bias[layer][None], gains[1], shifts[1], cotangent[0], inverse_one, gains[0]],
                [normed_one],
                [shape(tokens, width), *outs],
                1,
                saved,
                feeds[layer],
                squares[layer],
                wide,
                tokens,
            )
        else:
            normed_two, inverse_two, slope = kept_feed[layer]
            grad_one, query_grad, key_own, value_own, halo, prefix_parts[layer] = layer_call(
                back_kernel,
                (flag,),
                [gradient, near, across, edge, inverse_two, gains[1], inverse_one, gains[0]],
                [normed_two, slope, normed_one],
                outs,
                2,
                saved,
                feeds[layer],
                squares[layer],
                wide,
                tokens,
            )
        near = lax.ppermute(halo[:tokens], "keys", xor_pairs(places, 1))
        across = lax.ppermute(halo[tokens : 2 * tokens], "keys", [(1, 2), (2, 1)])
        edge = lax.ppermute(halo[2 * tokens :], "keys", xor_pairs(places, 2))
        gradient = input_back(grad_one, query_grad, key_own, value_own, squares[layer])
    extra = edge.astype(F32)
    lead = jnp.where(first_half, 0.0, extra)
    tail = jnp.where(first_half, extra, 0.0)
    gradient = (
        gradient
        + near.astype(F32)
        + across.astype(F32)
        + jnp.concatenate([lead, jnp.zeros((tokens - 2 * EDGE, width), F32), tail], 0)
    )
    prefix_total = sum_prefixes(jnp.stack(prefix_parts))
    return (
        result[None],
        gradient[None],
        prefix_total[:, 0],
        prefix_total[:, 1],
    )


def solution(mesh):
    placed = (
        P("rows", "keys", None),
        P("rows", None),
        P(None, "keys", None),
        P(None, "keys", None),
        P(None, "rows", None),
        P(None, "rows", None),
        P(None, "rows", None),
        P(None, "rows", None),
        P(None, "rows", None),
        P(),
        P(None, "rows", None),
        P(),
        P(),
        P("rows", "keys", None),
    )
    return jax.shard_map(
        body,
        mesh=mesh,
        in_specs=placed,
        out_specs=(
            P("rows", "keys", None),
            P("rows", "keys", None),
            P(None, "keys", None),
            P(None, "keys", None),
        ),
        check_vma=False,
    )
```

```python
from functools import partial

import jax
import jax.numpy as jnp
import numpy as np
from jax import lax
from jax.experimental import pallas as pl
from jax.experimental.pallas import tpu as pltpu
from jax.sharding import PartitionSpec as P

H = 16
HD = 64
LAYERS = 2
PAIRS = H // 2
EDGE = 32
LANES = 256
NORM_EPSILON = 1e-05
MASKED_SCORE = -1000000000.0
SCORE_SCALE = 0.125
F32 = jnp.float32
BF16 = jnp.bfloat16
MIB = 1 << 20


def nn(a, b):
    return lax.dot_general(a, b, (((1,), (0,)), ((), ())), preferred_element_type=F32)


def nt(a, b):
    return lax.dot_general(a, b, (((1,), (1,)), ((), ())), preferred_element_type=F32)


def ds(start, size):
    return pl.ds(pl.multiple_of(start, size), size)


def layer_norm(hidden, gain, shift):
    centered = hidden - jnp.mean(hidden, -1, keepdims=True)
    inverse = lax.rsqrt(jnp.mean(centered * centered, -1, keepdims=True) + NORM_EPSILON)
    normed = centered * inverse
    return normed * gain + shift, normed, inverse


def norm_back(grad_out, gain, normed, inverse):
    scaled = grad_out * gain
    return inverse * (
        scaled
        - jnp.mean(scaled, -1, keepdims=True)
        - normed * jnp.mean(scaled * normed, -1, keepdims=True)
    )


class Loads:
    def __init__(self, sems):
        self.sems, self.copies, self.count = sems, {}, 0

    def start(self, name, source, target):
        copy = pltpu.make_async_copy(source, target, self.sems.at[self.count])
        copy.start()
        self.copies[name] = copy
        self.count += 1

    def wait(self, *names):
        for name in names:
            if name in self.copies:
                self.copies.pop(name).wait()


def square(ref, columns=slice(None)):
    block = ref[:, :, columns]
    return block.reshape(block.shape[0] * block.shape[1], block.shape[2])


def load_attention(loads, gathered, start, kinds, weights):
    for i, kind in enumerate(kinds):
        loads.start(("square", kind), gathered.at[:, kind, start], weights.at[i])


def load_up(loads, gathered, start, up):
    each = up.shape[0] // (gathered.shape[1] // 2)
    for b in range(up.shape[0]):
        loads.start(("up", b), gathered.at[:, b // each, start + b % each], up.at[b])


def load_down(loads, gathered, start, down):
    half, each = down.shape[1:3]
    for r in range(down.shape[0]):
        loads.start(("down", r), gathered.at[r, pl.ds(half, half), pl.ds(start, each)], down.at[r])


def pair_blocks(half):
    zero = jnp.zeros((HD, LANES), half.dtype)
    return jnp.concatenate(
        [
            jnp.concatenate([half[:HD], zero], 1),
            jnp.concatenate([zero, half[HD:]], 1),
        ],
        0,
    )


def attention_kernel(start, *refs):
    (gathered, own, near, across, edge, residual, bias, prefix_k, prefix_v, gain, shift) = refs[:11]
    (middle, normed, inverse, query_t, value8, key_t, attend, heads_t) = refs[11:19]
    (weights, window, key8, value_t, scores, sems) = refs[19:]
    tokens, width = own.shape
    keys = key8.shape[1]
    loads = Loads(sems)
    load_attention(loads, gathered, start, range(4), weights)
    window[pl.ds(0, tokens)] = own[...]
    window[pl.ds(tokens, tokens)] = near[...]
    window[pl.ds(2 * tokens, tokens)] = across[...]
    window[pl.ds(3 * tokens, EDGE)] = edge[...]
    pad = jnp.zeros((LANES - tokens, 256), BF16)
    for kind in range(3):
        loads.wait(("square", kind))

    def tile(j, carry):
        columns = ds(j * 256, 256)
        query = (SCORE_SCALE * nn(own[...], square(weights.at[0], columns))).astype(BF16)
        query_t[columns, :] = jnp.concatenate([query, pad], 0).T
        for kind, prefix, split, turned in ((1, prefix_k, key8, key_t), (2, prefix_v, value8, value_t)):
            local = nn(window[...], square(weights.at[kind], columns)).astype(BF16)
            whole = jnp.concatenate([local, prefix[:, columns]], 0)
            split[2 * j] = whole[:, :128]
            split[2 * j + 1] = whole[:, 128:]
            turned[columns, :] = whole.T
        return carry

    lax.fori_loop(0, width // 256, tile, 0, unroll=2)
    wide = jnp.zeros((1, 2 * LANES), F32)
    step = 128

    def pair(p, carry):
        blocks = pair_blocks(query_t[ds(p * 128, 128), :])
        top = wide + 2 * MASKED_SCORE
        for c in range(0, keys, step):
            part = nn(key8[p, pl.ds(c, step), :], blocks)
            mask = bias[pl.ds(c, step), :]
            part = part + jnp.concatenate([mask, mask], 1)
            scores[pl.ds(c, step), :] = part
            top = jnp.maximum(top, jnp.max(part, 0, keepdims=True))
        total = wide
        for c in range(0, keys, step):
            part = jnp.exp(scores[pl.ds(c, step), :] - top)
            scores[pl.ds(c, step), :] = part
            total = total + jnp.sum(part, 0, keepdims=True)
        scale = 1.0 / total
        for c in range(0, keys, step):
            attend[p, pl.ds(c, step), :] = (scores[pl.ds(c, step), :] * scale).astype(BF16)
        for half in range(2):
            rows = pl.ds(pl.multiple_of(p * 128 + half * HD, HD), HD)
            heads_t[rows, :] = nn(value_t[rows, :], attend[p, :, pl.ds(half * LANES, LANES)])
        return carry

    lax.fori_loop(0, PAIRS, pair, 0)
    loads.wait(("square", 3))
    heads = heads_t[...].astype(BF16).T[:tokens]
    for c in range(0, width, 512):
        columns = pl.ds(c, 512)
        middle[:, columns] = residual[:, columns] + nn(heads, square(weights.at[3], columns))
    result, n, r = layer_norm(middle[...], gain[...], shift[...])
    middle[...] = result
    normed[...] = n
    inverse[...] = r


def feed_forward_steps(loads, middle, up_bias, gain, shift, up, down, low, hidden, slope, output):
    tokens, width = middle.shape
    low[pl.ds(0, tokens), :] = middle[...].astype(BF16)
    for b in range(up.shape[0]):
        loads.wait(("up", b))
        for c in range(0, width, 512):
            place = pl.ds(b * width + c, 512)
            u = nn(low[pl.ds(0, tokens), :], square(up.at[b], pl.ds(c, 512))) + up_bias[:, place]
            part = 0.5 + 0.5 * lax.erf(u * (0.5**0.5))
            hidden[:, place] = (u * part).astype(BF16)
            slope[:, place] = (part + u * (jnp.exp(-0.5 * u * u) * ((2 * np.pi) ** -0.5))).astype(BF16)
    for r in range(down.shape[0]):
        loads.wait(("down", r))
    for c in range(0, width, 512):
        columns = pl.ds(c, 512)
        block = down[:, :, :, :, columns].reshape(hidden.shape[1], 512)
        output[:, columns] = middle[:, columns] + nn(hidden[...], block)
    return layer_norm(output[...], gain[...], shift[...])


def forward_kernel(start, *refs):
    (gathered, middle, up_bias, gain, shift) = refs[:5]
    (output, low, normed, inverse, slope) = refs[5:10]
    (up, down, hidden, sems) = refs[10:]
    loads = Loads(sems)
    load_up(loads, gathered, start, up)
    load_down(loads, gathered, start, down)
    result, n, r = feed_forward_steps(loads, middle, up_bias, gain, shift, up, down, low, hidden, slope, output)
    output[...] = result
    low[...] = result.astype(BF16)
    normed[...] = n
    inverse[...] = r


def feed_back_steps(loads, grad_two, slope, normed_one, inverse_one, gain_one, up, down, weights, low, hidden, grad_one, heads_grad, grad_out):
    tokens, width = grad_two.shape
    low[pl.ds(0, tokens), :] = grad_two.astype(BF16)
    grad_one[...] = grad_two
    size = hidden.shape[1] // down.shape[0]
    for r in range(down.shape[0]):
        loads.wait(("down", r))
        place = pl.ds(r * size, size)
        back = nt(low[pl.ds(0, tokens), :], down[r].reshape(size, width))
        hidden[:, place] = (back * slope[:, place].astype(F32)).astype(BF16)
    rows = up.shape[2]
    for b in range(0, up.shape[0], 2):
        loads.wait(("up", b), ("up", b + 1))
        for c in range(0, width, 512):
            total = grad_one[:, pl.ds(c, 512)]
            for i in (b, b + 1):
                block = up[i, pl.ds(c // rows, 512 // rows)].reshape(512, width)
                total = total + nt(hidden[:, pl.ds(i * width, width)], block)
            grad_one[:, pl.ds(c, 512)] = total
    loads.wait("normed_one")
    back = norm_back(grad_one[...], gain_one[...], normed_one[...], inverse_one[...])
    grad_one[...] = back
    loads.start("grad_out", grad_one, grad_out)
    low[pl.ds(0, tokens), :] = back.astype(BF16)
    low[pl.ds(tokens, LANES - tokens), :] = jnp.zeros((LANES - tokens, width), BF16)
    loads.wait(("square", 3))
    heads_grad[...] = nt(square(weights.at[0]), low[...]).astype(BF16)


def attention_back_steps(loads, heads_grad, heads_t, query_t, value8, key_t, attend, weights, key_grad, value_grad, query_grad_t, query_rows, steps, outs):
    (query_grad, key_own, value_own, near_grad, across_grad, edge_grad, prefix_grad) = outs
    tokens, width = query_rows.shape
    keys = attend.shape[1]
    span = keys - prefix_grad.shape[1]
    loads.wait("low_out")
    loads.wait("heads_t", "query_t", "value8", "key_t")
    step = 128
    for p in range(PAIRS):
        loads.wait(("attend", p))
        rows = pl.ds(p * 128, 128)
        grad_t = heads_grad[rows, :]
        product = grad_t.astype(F32) * heads_t[rows, :]
        dots = jnp.concatenate(
            [jnp.sum(product[:HD], 0, keepdims=True), jnp.sum(product[HD:], 0, keepdims=True)], 1
        )
        blocks = pair_blocks(grad_t)
        grad_v = nt(attend[p], blocks)
        value_grad[:, rows] = grad_v.astype(BF16)
        prefix_grad[1, :, rows] = grad_v[span:]
        here = steps.at[p % 2]
        for c in range(0, keys, step):
            part = nn(value8[p, pl.ds(c, step), :], blocks) - dots
            here[pl.ds(c, step), :] = (attend[p, pl.ds(c, step), :].astype(F32) * part).astype(BF16)
        grad_k = nt(here[...], pair_blocks(query_t[rows, :]))
        key_grad[:, rows] = grad_k.astype(BF16)
        prefix_grad[0, :, rows] = grad_k[span:]
        for half in range(2):
            place = pl.ds(p * 128 + half * HD, HD)
            query_grad_t[place, :] = nn(key_t[place, :], here[:, pl.ds(half * LANES, LANES)]).astype(BF16)
    query_rows[...] = query_grad_t[...].T[:tokens]
    loads.start("query_out", query_rows, query_grad)
    loads.start("key_out", key_grad.at[pl.ds(0, tokens)], key_own)
    loads.start("value_out", value_grad.at[pl.ds(0, tokens)], value_own)
    loads.wait(("square", 1), ("square", 2))
    outer = pl.ds(tokens, span - tokens)
    rows = weights.shape[2]
    for c in range(0, width, 512):
        part = pl.ds(c // rows, 512 // rows)
        outer_grad = (
            nt(key_grad[outer, :], weights[1, part].reshape(512, width))
            + nt(value_grad[outer, :], weights[2, part].reshape(512, width))
        ).astype(BF16)
        near_grad[:, pl.ds(c, 512)] = outer_grad[:tokens]
        across_grad[:, pl.ds(c, 512)] = outer_grad[tokens : 2 * tokens]
        edge_grad[pl.ds(0, EDGE), pl.ds(c, 512)] = outer_grad[2 * tokens :]
    loads.wait("grad_out", "query_out", "key_out", "value_out")


def load_saved(loads, gathered, start, saved, weights, buffers):
    load_attention(loads, gathered, start, [3], weights.at[pl.ds(0, 1)])
    for name, source, target in zip(("heads_t", "query_t", "value8", "key_t"), saved, buffers):
        loads.start(name, source, target)
    for p in range(PAIRS):
        loads.start(("attend", p), saved[4].at[p], buffers[4].at[p])
    load_attention(loads, gathered, start, [1, 2], weights.at[pl.ds(1, 2)])


def input_back_steps(loads, weights, grad_one, sides, grad_input):
    width = grad_one.shape[1]
    rows = weights.shape[2]
    for kind in range(3):
        loads.wait(("side", kind), ("square", kind))
        before = grad_one if kind == 0 else grad_input
        for c in range(0, width, 512):
            columns = pl.ds(c, 512)
            part = nt(sides[kind], weights[kind, pl.ds(c // rows, 512 // rows)].reshape(512, width))
            grad_input[:, columns] = before[:, columns] + (SCORE_SCALE * part if kind == 0 else part)


def last_kernel(feed_start, attention_start, *refs):
    (feed, squares, middle, up_bias, gain_two, shift_two, cotangent, inverse_one, gain_one) = refs[:9]
    normed_hbm, saved = refs[9], refs[10:15]
    low_out, grad_out = refs[15:17]
    outs = refs[17:24]
    (up, down, weights, slope, low, hidden, grad_one, query_rows, normed_one, heads_grad) = refs[24:34]
    buffers = refs[34:39]
    (key_grad, value_grad, query_grad_t, steps, sems) = refs[39:]
    loads = Loads(sems)
    load_up(loads, feed, feed_start, up)
    load_down(loads, feed, feed_start, down)
    loads.start("normed_one", normed_hbm, normed_one)
    load_saved(loads, squares, attention_start, saved, weights, buffers)
    result, n, r = feed_forward_steps(
        loads, middle, up_bias, gain_two, shift_two, up, down, low, hidden, slope, grad_one
    )
    query_rows[...] = result.astype(BF16)
    loads.start("low_out", query_rows, low_out)
    grad_two = norm_back(cotangent[...].astype(F32), gain_two[...], n, r)
    feed_back_steps(
        loads, grad_two, slope, normed_one, inverse_one, gain_one, up, down, weights, low, hidden, grad_one, heads_grad, grad_out
    )
    attention_back_steps(
        loads, heads_grad, *buffers[:5], weights, key_grad, value_grad, query_grad_t, query_rows, steps, outs
    )


def back_kernel(feed_start, attention_start, *refs):
    (flag, feed, squares) = refs[:3]
    (grad, near, across, edge, inverse_two, gain_two, inverse_one, gain_one, prefix_after) = refs[3:12]
    (normed_two_hbm, slope_hbm, normed_one_hbm) = refs[12:15]
    saved = refs[15:20]
    grad_out = refs[20]
    outs = refs[21:27]
    edge_grad, prefix_kept = refs[26:28]
    (up, down, weights, slope, low, hidden, grad_one, query_rows, normed_two, normed_one, heads_grad) = refs[28:39]
    buffers = refs[39:44]
    (key_grad, value_grad, query_grad_t, steps, prefix_grad, sems) = refs[44:]
    tokens, width = grad_one.shape
    loads = Loads(sems)
    loads.start("normed_two", normed_two_hbm, normed_two)
    loads.start("slope", slope_hbm, slope)
    load_down(loads, feed, feed_start, down)
    load_up(loads, feed, feed_start, up)
    loads.start("normed_one", normed_one_hbm, normed_one)
    load_saved(loads, squares, attention_start, saved, weights, buffers)
    grad_one[...] = grad[...] + near[...].astype(F32) + across[...].astype(F32)
    last = flag[0].astype(F32)
    extra = edge[...].astype(F32)
    head, tail = pl.ds(0, EDGE), pl.ds(tokens - EDGE, EDGE)
    grad_one[head, :] = grad_one[head, :] + extra * (1.0 - last)
    grad_one[tail, :] = grad_one[tail, :] + extra * last
    loads.wait("normed_two")
    grad_two = norm_back(grad_one[...], gain_two[...], normed_two[...], inverse_two[...])
    loads.wait("slope")
    feed_back_steps(
        loads, grad_two, slope, normed_one, inverse_one, gain_one, up, down, weights, low, hidden, grad_one, heads_grad, grad_out
    )
    attention_back_steps(
        loads, heads_grad, *buffers[:5], weights, key_grad, value_grad, query_grad_t, query_rows, steps, (*outs, prefix_grad)
    )
    half = prefix_kept.shape[1]
    mine = 1 - flag[0]
    for layer, part in enumerate((prefix_grad, prefix_after)):
        for i in range(2):
            at = 2 * layer + i
            prefix_kept[at] = part[i, ds(mine * half, half), :]
            edge_grad[pl.ds(EDGE + at * half, half), :] = part[i, ds((1 - mine) * half, half), :].astype(BF16)


def input_back_kernel(start, through, *refs):
    (gathered, grad_hbm, query_hbm, key_hbm, value_hbm) = refs[:5]
    (grad_input, weights, grad_one, sides, sems) = refs[5 + 2 * through :]
    loads = Loads(sems)
    loads.start("grad", grad_hbm, grad_one)
    for kind, source in enumerate((query_hbm, key_hbm, value_hbm)):
        loads.start(("side", kind), source, sides.at[kind])
        load_attention(loads, gathered, start, [kind], weights.at[pl.ds(kind, 1)])
    loads.wait("grad")
    input_back_steps(loads, weights, grad_one, sides, grad_input)


def pack_kernel(place, query, key, value, out, up, down, first, second, sems):
    places = 4
    half = places // 2
    rows = query.shape[1]
    width = query.shape[2]
    each = second.shape[0]
    for k in range(places):

        @pl.when(place[0] == k)
        def _():
            matrix = (query, key, value, out)[k]
            jobs = [(matrix.at[0], first.at[0]), (matrix.at[1], first.at[each + 1])]
            for layer, target, begin in ((0, first, 1), (1, second, 0)):
                for i in range(each):
                    b = k * each + i
                    if k < half:
                        source = up.at[layer, :, pl.ds(b * width, width)]
                    else:
                        source = down.at[layer, pl.ds((b - half * each) * rows, rows)]
                    jobs.append((source, target.at[begin + i]))
            copies = [pltpu.make_async_copy(a, b, sems.at[i]) for i, (a, b) in enumerate(jobs)]
            for copy in copies:
                copy.start()
            for copy in copies:
                copy.wait()


VMEM = pl.BlockSpec(memory_space=pltpu.VMEM)
SMEM = pl.BlockSpec(memory_space=pltpu.SMEM)
ANY = pl.BlockSpec(memory_space=pl.ANY)
HBM = pl.BlockSpec(memory_space=pltpu.HBM)


def call(kernel, numbers, kept, operands, late, outs, scratch, limit, flops, sem_count, small=(), copied=0, aliases={}):
    moved = sum(x.size * x.dtype.itemsize for x in (*operands, *late)) + 16 * MIB
    return pl.pallas_call(
        partial(kernel, *numbers),
        out_shape=[shape(*x.shape, dtype=x.dtype) for x in outs],
        input_output_aliases=aliases,
        in_specs=[SMEM] * len(small) + [ANY] * len(kept) + [VMEM] * len(operands) + [ANY] * len(late),
        out_specs=[HBM] * copied + [VMEM] * (len(outs) - copied),
        scratch_shapes=[*scratch, pltpu.SemaphoreType.DMA((sem_count,))],
        compiler_params=pltpu.CompilerParams(vmem_limit_bytes=limit * MIB),
        cost_estimate=pl.CostEstimate(flops=flops, bytes_accessed=moved, transcendentals=0),
    )(*small, *kept, *operands, *late)


def shape(*sizes, dtype=BF16):
    return jax.ShapeDtypeStruct(sizes, dtype)


def feed_shapes(gathered, wide):
    parts, places, _, rows, width = gathered.shape
    ratio = wide // width
    return [shape(ratio, parts, rows, width), shape(parts, places // 2, 2 * ratio // places, rows, width)]


def squares_scratch(gathered, count):
    parts, _, _, rows, width = gathered.shape
    return pltpu.VMEM((count, parts, rows, width), BF16)


def attention_forward(inputs, inputs_low, around, bias, prefix_k, prefix_v, gain, shift, weights):
    gathered, start = weights
    tokens, width = inputs.shape
    keys = bias.shape[0]
    span = keys - prefix_k.shape[0]
    return call(
        attention_kernel,
        [start],
        [gathered],
        [inputs_low, *around, inputs, bias, prefix_k, prefix_v, gain, shift],
        [],
        [
            shape(tokens, width, dtype=F32),
            shape(tokens, width, dtype=F32),
            shape(tokens, 1, dtype=F32),
            shape(width, LANES),
            shape(PAIRS, keys, 128),
            shape(width, keys),
            shape(PAIRS, keys, 2 * LANES),
            shape(width, LANES, dtype=F32),
        ],
        [
            squares_scratch(gathered, 4),
            pltpu.VMEM((span, width), BF16),
            pltpu.VMEM((PAIRS, keys, 128), BF16),
            pltpu.VMEM((width, keys), BF16),
            pltpu.VMEM((keys, 2 * LANES), F32),
        ],
        40,
        2 * tokens * width * width * 8,
        4,
    )


def feed_forward(middle, up_bias, gain, shift, weights):
    gathered, start = weights
    tokens, width = middle.shape
    wide = up_bias.shape[1]
    return call(
        forward_kernel,
        [start],
        [gathered],
        [middle, up_bias, gain, shift],
        [],
        [
            shape(tokens, width, dtype=F32),
            shape(tokens, width),
            shape(tokens, width, dtype=F32),
            shape(tokens, 1, dtype=F32),
            shape(tokens, wide),
        ],
        [*[pltpu.VMEM(x.shape, BF16) for x in feed_shapes(gathered, wide)], pltpu.VMEM((tokens, wide), BF16)],
        40,
        4 * tokens * width * wide,
        wide // width + gathered.shape[0],
    )


def back_shapes(tokens, width):
    return [
        shape(tokens, width, dtype=F32),
        shape(tokens, width),
        shape(tokens, width),
        shape(tokens, width),
        shape(tokens, width),
        shape(tokens, width),
        shape(EDGE, width),
    ]


def saved_scratch(saved):
    heads_t, query_t, value8, key_t, attend = saved
    keys = attend.shape[1]
    width = heads_t.shape[0]
    return [pltpu.VMEM(x.shape, x.dtype) for x in saved] + [
        pltpu.VMEM((keys, width), BF16),
        pltpu.VMEM((keys, width), BF16),
        pltpu.VMEM((width, LANES), BF16),
        pltpu.VMEM((2, keys, 2 * LANES), BF16),
    ]


def layer_call(kernel, numbers, small, kept, operands, late, outs, copied, kinds, saved, wide, tokens, limit, extra=()):
    parts, _, _, _, width = kept[0].shape
    return call(
        kernel,
        numbers,
        kept,
        operands,
        [*late, *saved],
        outs,
        [
            *[pltpu.VMEM(x.shape, BF16) for x in feed_shapes(kept[0], wide)],
            squares_scratch(kept[0], 3),
            pltpu.VMEM((tokens, wide), BF16),
            pltpu.VMEM((LANES, width), BF16),
            pltpu.VMEM((tokens, wide), BF16),
            pltpu.VMEM((tokens, width), F32),
            pltpu.VMEM((tokens, width), BF16),
            *[pltpu.VMEM((tokens, width), F32)] * kinds,
            pltpu.VMEM((width, LANES), BF16),
            *saved_scratch(saved),
            *extra,
        ],
        limit,
        8 * tokens * width * wide,
        wide // width + parts + 3 + 4 + PAIRS + 6 + 9,
        small,
        copied,
    )


def input_back(grad_one, query_grad, key_own, value_own, weights, through=()):
    gathered, start = weights
    tokens, width = grad_one.shape
    outs = call(
        input_back_kernel,
        [start, len(through)],
        [gathered],
        [],
        [grad_one, query_grad, key_own, value_own, *through],
        [*through, shape(tokens, width, dtype=F32)],
        [squares_scratch(gathered, 3), pltpu.VMEM((tokens, width), F32), pltpu.VMEM((3, tokens, width), BF16)],
        30,
        6 * tokens * width * width,
        7,
        (),
        len(through),
        {5 + i: i for i in range(len(through))},
    )
    return outs[-1], *outs[:-1]


def pack(place, w_query, w_key, w_value, w_out, w_up, w_down, each):
    rows, width = w_query.shape[1:]
    return pl.pallas_call(
        pack_kernel,
        out_shape=[shape(each + 2, rows, width), shape(each, rows, width)],
        in_specs=[SMEM] + [ANY] * 6,
        out_specs=[VMEM] * 2,
        scratch_shapes=[pltpu.SemaphoreType.DMA((2 * each + 2,))],
    )(place, w_query, w_key, w_value, w_out, w_up, w_down)


def xor_pairs(count, bit):
    return [(i, i ^ bit) for i in range(count)]


def sum_prefixes(total):
    place = lax.axis_index("keys")
    places = lax.axis_size("keys")
    step = places // 4
    while step:
        split = total.reshape(total.shape[0], 2, -1, total.shape[2])
        mine = (place // step) % 2
        sent = lax.dynamic_index_in_dim(split, 1 - mine, 1, False).astype(BF16)
        kept = lax.dynamic_index_in_dim(split, mine, 1, False)
        total = kept + lax.ppermute(sent, "keys", xor_pairs(places, step)).astype(F32)
        step //= 2
    count = lax.axis_size("rows")
    step = 1
    while step < count:
        total = total + lax.ppermute(total.astype(BF16), "rows", xor_pairs(count, step)).astype(F32)
        step *= 2
    return total


def body(
    activations,
    segments,
    prefix_keys,
    prefix_values,
    w_query,
    w_key,
    w_value,
    w_out,
    w_up,
    ff_bias,
    w_down,
    ln_gain,
    ln_bias,
    cotangent,
):
    _, tokens, width = activations.shape
    wide = w_up.shape[2]
    ratio = wide // width
    places = lax.axis_size("keys")
    parts = lax.axis_size("rows")
    rows = width // parts
    place = lax.axis_index("keys")
    prefix = prefix_keys.shape[1] * places
    first_half = place < places // 2

    each = 2 * ratio // places
    shares = pack(place[None], w_query, w_key, w_value, w_out, w_up, w_down, each)

    def gather(share):
        whole = lax.all_gather(share, ("rows", "keys"), axis=0, tiled=True)
        return whole.reshape(parts, places, share.shape[0], rows, width)

    first, second = gather(shares[0]), gather(shares[1])
    squares = [(first, 0), (first, each + 1)]
    feeds = [(first, 1), (second, 0)]

    def exchange(low):
        near = lax.ppermute(low, "keys", xor_pairs(places, 1))
        across = lax.ppermute(low, "keys", [(1, 2), (2, 1)])
        edge = lax.ppermute(
            jnp.where(first_half, low[tokens - EDGE :], low[:EDGE]), "keys", xor_pairs(places, 2)
        )
        return near, across, edge

    def send_halo(halo):
        near = lax.ppermute(halo[0], "keys", xor_pairs(places, 1))
        across = lax.ppermute(halo[1], "keys", [(1, 2), (2, 1)])
        edge = lax.ppermute(halo[2], "keys", xor_pairs(places, 2))
        return near, across, edge

    line = segments[0]

    def ids(where, start, size):
        return lax.dynamic_slice_in_dim(line, where * tokens + start, size, 0)

    own_ids = ids(place, 0, tokens)
    across_ids = jnp.where(
        (place == 1) | (place == 2), ids(jnp.clip(3 - place, 0, places - 1), 0, tokens), -1
    )
    edge_ids = ids(place ^ 2, jnp.where(first_half, 0, tokens - EDGE), EDGE)
    key_ids = jnp.concatenate([own_ids, ids(place ^ 1, 0, tokens), across_ids, edge_ids])
    allowed = jnp.concatenate([key_ids[:, None] == own_ids[None, :], jnp.ones((prefix, tokens), bool)], 0)
    bias = jnp.pad(jnp.where(allowed, 0.0, MASKED_SCORE).astype(F32), ((0, 0), (0, LANES - tokens)))

    prefixes = lax.all_gather(jnp.stack([prefix_keys, prefix_values]), "keys", axis=2, tiled=True)

    low = activations[0]
    hidden = low.astype(F32)
    kept = []
    for layer in range(LAYERS):
        gains, shifts = ln_gain[layer][:, None], ln_bias[layer][:, None]
        around = exchange(low)
        middle, normed_one, inverse_one, query_t, value8, key_t, attend, heads_t = attention_forward(
            hidden,
            low,
            around,
            bias,
            prefixes[0, layer],
            prefixes[1, layer],
            gains[0],
            shifts[0],
            squares[layer],
        )
        saved = (heads_t, query_t, value8, key_t, attend)
        kept.append(((normed_one, inverse_one), saved))
        if layer < LAYERS - 1:
            hidden, low, *second_norm = feed_forward(middle, ff_bias[layer][None], gains[1], shifts[1], feeds[layer])

    flag = first_half.astype(jnp.int32)[None]
    back = back_shapes(tokens, width)
    both = shape(2, prefix, width, dtype=F32)
    (normed_one, inverse_one), saved = kept[1]
    gains, shifts = ln_gain[1][:, None], ln_bias[1][:, None]
    result, grad_one, query_grad, key_own, value_own, *halo, prefix_after = layer_call(
        last_kernel,
        [feeds[1][1], squares[1][1]],
        (),
        [feeds[1][0], squares[1][0]],
        [middle, ff_bias[1][None], gains[1], shifts[1], cotangent[0], inverse_one, gains[0]],
        [normed_one],
        [shape(tokens, width), *back, both],
        5,
        1,
        saved,
        wide,
        tokens,
        52,
    )
    near, across, edge = send_halo(halo)
    (gradient,) = input_back(grad_one, query_grad, key_own, value_own, squares[1])
    (normed_one, inverse_one), saved = kept[0]
    normed_two, inverse_two, slope = second_norm
    gains = ln_gain[0][:, None]
    half = prefix // 2
    back[-1] = shape(EDGE + LAYERS * 2 * half, width)
    grad_one, query_grad, key_own, value_own, *halo, prefix_kept = layer_call(
        back_kernel,
        [feeds[0][1], squares[0][1]],
        (flag,),
        [feeds[0][0], squares[0][0]],
        [gradient, near, across, edge, inverse_two, gains[1], inverse_one, gains[0], prefix_after],
        [normed_two, slope, normed_one],
        [*back, shape(LAYERS * 2, half, width, dtype=F32)],
        4,
        2,
        saved,
        wide,
        tokens,
        50,
        [pltpu.VMEM(both.shape, F32)],
    )
    near, across, edge = send_halo(halo)
    gradient, prefix_kept = input_back(grad_one, query_grad, key_own, value_own, squares[0], [prefix_kept])
    prefix_total = sum_prefixes(prefix_kept + edge[EDGE:].reshape(LAYERS * 2, half, width).astype(F32))
    prefix_total = prefix_total.reshape(LAYERS, 2, prefix // places, width)
    edge = edge[:EDGE]
    extra = edge.astype(F32)
    lead = jnp.where(first_half, 0.0, extra)
    tail = jnp.where(first_half, extra, 0.0)
    gradient = (
        gradient
        + near.astype(F32)
        + across.astype(F32)
        + jnp.concatenate([lead, jnp.zeros((tokens - 2 * EDGE, width), F32), tail], 0)
    )
    return (
        result[None],
        gradient[None],
        prefix_total[:, 0],
        prefix_total[:, 1],
    )


def solution(mesh):
    placed = (
        P("rows", "keys", None),
        P("rows", None),
        P(None, "keys", None),
        P(None, "keys", None),
        P(None, "rows", None),
        P(None, "rows", None),
        P(None, "rows", None),
        P(None, "rows", None),
        P(None, "rows", None),
        P(),
        P(None, "rows", None),
        P(),
        P(),
        P("rows", "keys", None),
    )
    return jax.shard_map(
        body,
        mesh=mesh,
        in_specs=placed,
        out_specs=(
            P("rows", "keys", None),
            P("rows", "keys", None),
            P(None, "keys", None),
            P(None, "keys", None),
        ),
        check_vma=False,
    )
```

```python
from functools import partial

import jax
import jax.numpy as jnp
import numpy as np
from jax import lax
from jax.experimental import pallas as pl
from jax.experimental.pallas import tpu as pltpu
from jax.sharding import PartitionSpec as P

H = 16
HD = 64
LAYERS = 2
PAIRS = H // 2
EDGE = 32
LANES = 256
NORM_EPSILON = 1e-05
MASKED_SCORE = -1000000000.0
SCORE_SCALE = 0.125
F32 = jnp.float32
BF16 = jnp.bfloat16
MIB = 1 << 20


def nn(a, b):
    return lax.dot_general(a, b, (((1,), (0,)), ((), ())), preferred_element_type=F32)


def nt(a, b):
    return lax.dot_general(a, b, (((1,), (1,)), ((), ())), preferred_element_type=F32)


def ds(start, size):
    return pl.ds(pl.multiple_of(start, size), size)


def layer_norm(hidden, gain, shift):
    centered = hidden - jnp.mean(hidden, -1, keepdims=True)
    inverse = lax.rsqrt(jnp.mean(centered * centered, -1, keepdims=True) + NORM_EPSILON)
    normed = centered * inverse
    return normed * gain + shift, normed, inverse


def norm_back(grad_out, gain, normed, inverse):
    scaled = grad_out * gain
    return inverse * (
        scaled
        - jnp.mean(scaled, -1, keepdims=True)
        - normed * jnp.mean(scaled * normed, -1, keepdims=True)
    )


class Loads:
    def __init__(self, sems):
        self.sems, self.copies, self.count = sems, {}, 0

    def start(self, name, source, target):
        copy = pltpu.make_async_copy(source, target, self.sems.at[self.count])
        copy.start()
        self.copies[name] = copy
        self.count += 1

    def wait(self, *names):
        for name in names:
            if name in self.copies:
                self.copies.pop(name).wait()


def square(ref, columns=slice(None)):
    block = ref[:, :, columns]
    return block.reshape(block.shape[0] * block.shape[1], block.shape[2])


def load_attention(loads, gathered, start, kinds, weights):
    for i, kind in enumerate(kinds):
        loads.start(("square", kind), gathered.at[:, kind, start], weights.at[i])


def load_up(loads, gathered, start, up):
    each = up.shape[0] // (gathered.shape[1] // 2)
    for b in range(up.shape[0]):
        loads.start(("up", b), gathered.at[:, b // each, start + b % each], up.at[b])


def load_down(loads, gathered, start, down):
    half, each = down.shape[1:3]
    for r in range(down.shape[0]):
        loads.start(("down", r), gathered.at[r, pl.ds(half, half), pl.ds(start, each)], down.at[r])


def pair_blocks(half):
    zero = jnp.zeros((HD, LANES), half.dtype)
    return jnp.concatenate(
        [
            jnp.concatenate([half[:HD], zero], 1),
            jnp.concatenate([zero, half[HD:]], 1),
        ],
        0,
    )


def attention_kernel(start, *refs):
    (gathered, own, near, across, edge, residual, bias, prefix_k, prefix_v, gain, shift) = refs[:11]
    (middle, normed, inverse, query_t, value8, key_t, attend, heads_t) = refs[11:19]
    (weights, window, key8, value_t, scores, sems) = refs[19:]
    tokens, width = own.shape
    keys = key8.shape[1]
    loads = Loads(sems)
    load_attention(loads, gathered, start, range(4), weights)
    window[pl.ds(0, tokens)] = own[...]
    window[pl.ds(tokens, tokens)] = near[...]
    window[pl.ds(2 * tokens, tokens)] = across[...]
    window[pl.ds(3 * tokens, EDGE)] = edge[...]
    pad = jnp.zeros((LANES - tokens, 256), BF16)
    for kind in range(3):
        loads.wait(("square", kind))

    def tile(j, carry):
        columns = ds(j * 256, 256)
        query = (SCORE_SCALE * nn(own[...], square(weights.at[0], columns))).astype(BF16)
        query_t[columns, :] = jnp.concatenate([query, pad], 0).T
        for kind, prefix, split, turned in ((1, prefix_k, key8, key_t), (2, prefix_v, value8, value_t)):
            local = nn(window[...], square(weights.at[kind], columns)).astype(BF16)
            whole = jnp.concatenate([local, prefix[:, columns]], 0)
            split[2 * j] = whole[:, :128]
            split[2 * j + 1] = whole[:, 128:]
            turned[columns, :] = whole.T
        return carry

    lax.fori_loop(0, width // 256, tile, 0, unroll=2)
    wide = jnp.zeros((1, 2 * LANES), F32)
    step = 128

    def pair(p, carry):
        blocks = pair_blocks(query_t[ds(p * 128, 128), :])
        top = wide + 2 * MASKED_SCORE
        for c in range(0, keys, step):
            part = nn(key8[p, pl.ds(c, step), :], blocks)
            mask = bias[pl.ds(c, step), :]
            part = part + jnp.concatenate([mask, mask], 1)
            scores[pl.ds(c, step), :] = part
            top = jnp.maximum(top, jnp.max(part, 0, keepdims=True))
        total = wide
        for c in range(0, keys, step):
            part = jnp.exp(scores[pl.ds(c, step), :] - top)
            scores[pl.ds(c, step), :] = part
            total = total + jnp.sum(part, 0, keepdims=True)
        scale = 1.0 / total
        for c in range(0, keys, step):
            attend[p, pl.ds(c, step), :] = (scores[pl.ds(c, step), :] * scale).astype(BF16)
        for half in range(2):
            rows = pl.ds(pl.multiple_of(p * 128 + half * HD, HD), HD)
            heads_t[rows, :] = nn(value_t[rows, :], attend[p, :, pl.ds(half * LANES, LANES)])
        return carry

    lax.fori_loop(0, PAIRS, pair, 0)
    loads.wait(("square", 3))
    heads = heads_t[...].astype(BF16).T[:tokens]
    for c in range(0, width, 512):
        columns = pl.ds(c, 512)
        middle[:, columns] = residual[:, columns] + nn(heads, square(weights.at[3], columns))
    result, n, r = layer_norm(middle[...], gain[...], shift[...])
    middle[...] = result
    normed[...] = n
    inverse[...] = r


def feed_forward_steps(loads, middle, up_bias, gain, shift, up, down, low, hidden, slope, output):
    tokens, width = middle.shape
    low[pl.ds(0, tokens), :] = middle[...].astype(BF16)
    for b in range(up.shape[0]):
        loads.wait(("up", b))
        for c in range(0, width, 512):
            place = pl.ds(b * width + c, 512)
            u = nn(low[pl.ds(0, tokens), :], square(up.at[b], pl.ds(c, 512))) + up_bias[:, place]
            part = 0.5 + 0.5 * lax.erf(u * (0.5**0.5))
            hidden[:, place] = (u * part).astype(BF16)
            slope[:, place] = (part + u * (jnp.exp(-0.5 * u * u) * ((2 * np.pi) ** -0.5))).astype(BF16)
    for r in range(down.shape[0]):
        loads.wait(("down", r))
    for c in range(0, width, 512):
        columns = pl.ds(c, 512)
        block = down[:, :, :, :, columns].reshape(hidden.shape[1], 512)
        output[:, columns] = middle[:, columns] + nn(hidden[...], block)
    return layer_norm(output[...], gain[...], shift[...])


def forward_kernel(start, *refs):
    (gathered, middle, up_bias, gain, shift) = refs[:5]
    (output, low, normed, inverse, slope) = refs[5:10]
    (up, down, hidden, sems) = refs[10:]
    loads = Loads(sems)
    load_up(loads, gathered, start, up)
    load_down(loads, gathered, start, down)
    result, n, r = feed_forward_steps(loads, middle, up_bias, gain, shift, up, down, low, hidden, slope, output)
    output[...] = result
    low[...] = result.astype(BF16)
    normed[...] = n
    inverse[...] = r


def feed_back_steps(loads, grad_two, slope, normed_one, inverse_one, gain_one, up, down, weights, low, hidden, grad_one, heads_grad, grad_out):
    tokens, width = grad_two.shape
    low[pl.ds(0, tokens), :] = grad_two.astype(BF16)
    grad_one[...] = grad_two
    size = hidden.shape[1] // down.shape[0]
    for r in range(down.shape[0]):
        loads.wait(("down", r))
        place = pl.ds(r * size, size)
        back = nt(low[pl.ds(0, tokens), :], down[r].reshape(size, width))
        hidden[:, place] = (back * slope[:, place].astype(F32)).astype(BF16)
    rows = up.shape[2]
    for b in range(0, up.shape[0], 2):
        loads.wait(("up", b), ("up", b + 1))
        for c in range(0, width, 512):
            total = grad_one[:, pl.ds(c, 512)]
            for i in (b, b + 1):
                block = up[i, pl.ds(c // rows, 512 // rows)].reshape(512, width)
                total = total + nt(hidden[:, pl.ds(i * width, width)], block)
            grad_one[:, pl.ds(c, 512)] = total
    loads.wait("normed_one")
    back = norm_back(grad_one[...], gain_one[...], normed_one[...], inverse_one[...])
    grad_one[...] = back
    loads.start("grad_out", grad_one, grad_out)
    low[pl.ds(0, tokens), :] = back.astype(BF16)
    low[pl.ds(tokens, LANES - tokens), :] = jnp.zeros((LANES - tokens, width), BF16)
    loads.wait(("square", 3))
    heads_grad[...] = nt(square(weights.at[0]), low[...]).astype(BF16)


def attention_back_steps(loads, heads_grad, heads_t, query_t, value8, key_t, attend, weights, key_grad, value_grad, query_grad_t, query_rows, steps, outs):
    (query_grad, key_own, value_own, near_grad, across_grad, edge_grad, prefix_grad) = outs
    tokens, width = query_rows.shape
    keys = attend.shape[1]
    span = keys - prefix_grad.shape[1]
    loads.wait("low_out")
    loads.wait("heads_t", "query_t", "value8", "key_t")
    step = 128
    for p in range(PAIRS):
        loads.wait(("attend", p))
        rows = pl.ds(p * 128, 128)
        grad_t = heads_grad[rows, :]
        product = grad_t.astype(F32) * heads_t[rows, :]
        dots = jnp.concatenate(
            [jnp.sum(product[:HD], 0, keepdims=True), jnp.sum(product[HD:], 0, keepdims=True)], 1
        )
        blocks = pair_blocks(grad_t)
        grad_v = nt(attend[p], blocks)
        value_grad[:, rows] = grad_v.astype(BF16)
        prefix_grad[1, :, rows] = grad_v[span:]
        here = steps.at[p % 2]
        for c in range(0, keys, step):
            part = nn(value8[p, pl.ds(c, step), :], blocks) - dots
            here[pl.ds(c, step), :] = (attend[p, pl.ds(c, step), :].astype(F32) * part).astype(BF16)
        grad_k = nt(here[...], pair_blocks(query_t[rows, :]))
        key_grad[:, rows] = grad_k.astype(BF16)
        prefix_grad[0, :, rows] = grad_k[span:]
        for half in range(2):
            place = pl.ds(p * 128 + half * HD, HD)
            query_grad_t[place, :] = nn(key_t[place, :], here[:, pl.ds(half * LANES, LANES)]).astype(BF16)
    query_rows[...] = query_grad_t[...].T[:tokens]
    loads.start("query_out", query_rows, query_grad)
    loads.start("key_out", key_grad.at[pl.ds(0, tokens)], key_own)
    loads.start("value_out", value_grad.at[pl.ds(0, tokens)], value_own)
    loads.wait(("square", 1), ("square", 2))
    outer = pl.ds(tokens, span - tokens)
    rows = weights.shape[2]
    for c in range(0, width, 512):
        part = pl.ds(c // rows, 512 // rows)
        outer_grad = (
            nt(key_grad[outer, :], weights[1, part].reshape(512, width))
            + nt(value_grad[outer, :], weights[2, part].reshape(512, width))
        ).astype(BF16)
        near_grad[:, pl.ds(c, 512)] = outer_grad[:tokens]
        across_grad[:, pl.ds(c, 512)] = outer_grad[tokens : 2 * tokens]
        edge_grad[pl.ds(0, EDGE), pl.ds(c, 512)] = outer_grad[2 * tokens :]
    loads.wait("grad_out", "query_out", "key_out", "value_out")


def load_saved(loads, gathered, start, saved, weights, buffers):
    load_attention(loads, gathered, start, [3], weights.at[pl.ds(0, 1)])
    for name, source, target in zip(("heads_t", "query_t", "value8", "key_t"), saved, buffers):
        loads.start(name, source, target)
    for p in range(PAIRS):
        loads.start(("attend", p), saved[4].at[p], buffers[4].at[p])
    load_attention(loads, gathered, start, [1, 2], weights.at[pl.ds(1, 2)])


def input_back_steps(loads, weights, grad_one, sides, grad_input):
    width = grad_one.shape[1]
    rows = weights.shape[2]
    for kind in range(3):
        loads.wait(("side", kind), ("square", kind))
        before = grad_one if kind == 0 else grad_input
        for c in range(0, width, 512):
            columns = pl.ds(c, 512)
            part = nt(sides[kind], weights[kind, pl.ds(c // rows, 512 // rows)].reshape(512, width))
            grad_input[:, columns] = before[:, columns] + (SCORE_SCALE * part if kind == 0 else part)


def last_kernel(feed_start, attention_start, *refs):
    (feed, squares, middle, up_bias, gain_two, shift_two, cotangent, inverse_one, gain_one) = refs[:9]
    normed_hbm, saved = refs[9], refs[10:15]
    low_out, grad_out = refs[15:17]
    outs = refs[17:24]
    (up, down, weights, slope, low, hidden, grad_one, query_rows, normed_one, heads_grad) = refs[24:34]
    buffers = refs[34:39]
    (key_grad, value_grad, query_grad_t, steps, sems) = refs[39:]
    loads = Loads(sems)
    load_up(loads, feed, feed_start, up)
    load_down(loads, feed, feed_start, down)
    loads.start("normed_one", normed_hbm, normed_one)
    load_saved(loads, squares, attention_start, saved, weights, buffers)
    result, n, r = feed_forward_steps(
        loads, middle, up_bias, gain_two, shift_two, up, down, low, hidden, slope, grad_one
    )
    query_rows[...] = result.astype(BF16)
    loads.start("low_out", query_rows, low_out)
    grad_two = norm_back(cotangent[...].astype(F32), gain_two[...], n, r)
    feed_back_steps(
        loads, grad_two, slope, normed_one, inverse_one, gain_one, up, down, weights, low, hidden, grad_one, heads_grad, grad_out
    )
    attention_back_steps(
        loads, heads_grad, *buffers[:5], weights, key_grad, value_grad, query_grad_t, query_rows, steps, outs
    )


def back_kernel(feed_start, attention_start, *refs):
    (flag, feed, squares) = refs[:3]
    (grad, near, across, edge, inverse_two, gain_two, inverse_one, gain_one, prefix_after) = refs[3:12]
    (normed_two_hbm, slope_hbm, normed_one_hbm) = refs[12:15]
    saved = refs[15:20]
    grad_out = refs[20]
    outs = refs[21:27]
    edge_grad, prefix_kept = refs[26:28]
    (up, down, weights, slope, low, hidden, grad_one, query_rows, normed_two, normed_one, heads_grad) = refs[28:39]
    buffers = refs[39:44]
    (key_grad, value_grad, query_grad_t, steps, prefix_grad, sems) = refs[44:]
    tokens, width = grad_one.shape
    loads = Loads(sems)
    loads.start("normed_two", normed_two_hbm, normed_two)
    loads.start("slope", slope_hbm, slope)
    load_down(loads, feed, feed_start, down)
    load_up(loads, feed, feed_start, up)
    loads.start("normed_one", normed_one_hbm, normed_one)
    load_saved(loads, squares, attention_start, saved, weights, buffers)
    grad_one[...] = grad[...] + near[...].astype(F32) + across[...].astype(F32)
    last = flag[0].astype(F32)
    extra = edge[...].astype(F32)
    head, tail = pl.ds(0, EDGE), pl.ds(tokens - EDGE, EDGE)
    grad_one[head, :] = grad_one[head, :] + extra * (1.0 - last)
    grad_one[tail, :] = grad_one[tail, :] + extra * last
    loads.wait("normed_two")
    grad_two = norm_back(grad_one[...], gain_two[...], normed_two[...], inverse_two[...])
    loads.wait("slope")
    feed_back_steps(
        loads, grad_two, slope, normed_one, inverse_one, gain_one, up, down, weights, low, hidden, grad_one, heads_grad, grad_out
    )
    attention_back_steps(
        loads, heads_grad, *buffers[:5], weights, key_grad, value_grad, query_grad_t, query_rows, steps, (*outs, prefix_grad)
    )
    half = prefix_kept.shape[1]
    mine = 1 - flag[0]
    for layer, part in enumerate((prefix_grad, prefix_after)):
        for i in range(2):
            at = 2 * layer + i
            prefix_kept[at] = part[i, ds(mine * half, half), :]
            edge_grad[pl.ds(EDGE + at * half, half), :] = part[i, ds((1 - mine) * half, half), :].astype(BF16)


def input_back_kernel(start, through, *refs):
    (gathered, grad_hbm, query_hbm, key_hbm, value_hbm) = refs[:5]
    (grad_input, weights, grad_one, sides, sems) = refs[5 + 2 * through :]
    loads = Loads(sems)
    loads.start("grad", grad_hbm, grad_one)
    for kind, source in enumerate((query_hbm, key_hbm, value_hbm)):
        loads.start(("side", kind), source, sides.at[kind])
        load_attention(loads, gathered, start, [kind], weights.at[pl.ds(kind, 1)])
    loads.wait("grad")
    input_back_steps(loads, weights, grad_one, sides, grad_input)


def pack_kernel(place, query, key, value, out, up, down, first, second, sems):
    places = 4
    half = places // 2
    rows = query.shape[1]
    width = query.shape[2]
    each = second.shape[0]
    for k in range(places):

        @pl.when(place[0] == k)
        def _():
            matrix = (query, key, value, out)[k]
            jobs = [(matrix.at[0], first.at[0]), (matrix.at[1], first.at[each + 1])]
            for layer, target, begin in ((0, first, 1), (1, second, 0)):
                for i in range(each):
                    b = k * each + i
                    if k < half:
                        source = up.at[layer, :, pl.ds(b * width, width)]
                    else:
                        source = down.at[layer, pl.ds((b - half * each) * rows, rows)]
                    jobs.append((source, target.at[begin + i]))
            copies = [pltpu.make_async_copy(a, b, sems.at[i]) for i, (a, b) in enumerate(jobs)]
            for copy in copies:
                copy.start()
            for copy in copies:
                copy.wait()


VMEM = pl.BlockSpec(memory_space=pltpu.VMEM)
SMEM = pl.BlockSpec(memory_space=pltpu.SMEM)
ANY = pl.BlockSpec(memory_space=pl.ANY)
HBM = pl.BlockSpec(memory_space=pltpu.HBM)


def call(kernel, numbers, kept, operands, late, outs, scratch, limit, flops, sem_count, small=(), copied=0, aliases={}):
    moved = sum(x.size * x.dtype.itemsize for x in (*operands, *late)) + 16 * MIB
    return pl.pallas_call(
        partial(kernel, *numbers),
        out_shape=[shape(*x.shape, dtype=x.dtype) for x in outs],
        input_output_aliases=aliases,
        in_specs=[SMEM] * len(small) + [ANY] * len(kept) + [VMEM] * len(operands) + [ANY] * len(late),
        out_specs=[HBM] * copied + [VMEM] * (len(outs) - copied),
        scratch_shapes=[*scratch, pltpu.SemaphoreType.DMA((sem_count,))],
        compiler_params=pltpu.CompilerParams(vmem_limit_bytes=limit * MIB),
        cost_estimate=pl.CostEstimate(flops=flops, bytes_accessed=moved, transcendentals=0),
    )(*small, *kept, *operands, *late)


def shape(*sizes, dtype=BF16):
    return jax.ShapeDtypeStruct(sizes, dtype)


def feed_shapes(gathered, wide):
    parts, places, _, rows, width = gathered.shape
    ratio = wide // width
    return [shape(ratio, parts, rows, width), shape(parts, places // 2, 2 * ratio // places, rows, width)]


def squares_scratch(gathered, count):
    parts, _, _, rows, width = gathered.shape
    return pltpu.VMEM((count, parts, rows, width), BF16)


def attention_forward(inputs, inputs_low, around, bias, prefix_k, prefix_v, gain, shift, weights):
    gathered, start = weights
    tokens, width = inputs.shape
    keys = bias.shape[0]
    span = keys - prefix_k.shape[0]
    return call(
        attention_kernel,
        [start],
        [gathered],
        [inputs_low, *around, inputs, bias, prefix_k, prefix_v, gain, shift],
        [],
        [
            shape(tokens, width, dtype=F32),
            shape(tokens, width, dtype=F32),
            shape(tokens, 1, dtype=F32),
            shape(width, LANES),
            shape(PAIRS, keys, 128),
            shape(width, keys),
            shape(PAIRS, keys, 2 * LANES),
            shape(width, LANES, dtype=F32),
        ],
        [
            squares_scratch(gathered, 4),
            pltpu.VMEM((span, width), BF16),
            pltpu.VMEM((PAIRS, keys, 128), BF16),
            pltpu.VMEM((width, keys), BF16),
            pltpu.VMEM((keys, 2 * LANES), F32),
        ],
        40,
        2 * tokens * width * width * 8,
        4,
    )


def feed_forward(middle, up_bias, gain, shift, weights):
    gathered, start = weights
    tokens, width = middle.shape
    wide = up_bias.shape[1]
    return call(
        forward_kernel,
        [start],
        [gathered],
        [middle, up_bias, gain, shift],
        [],
        [
            shape(tokens, width, dtype=F32),
            shape(tokens, width),
            shape(tokens, width, dtype=F32),
            shape(tokens, 1, dtype=F32),
            shape(tokens, wide),
        ],
        [*[pltpu.VMEM(x.shape, BF16) for x in feed_shapes(gathered, wide)], pltpu.VMEM((tokens, wide), BF16)],
        40,
        4 * tokens * width * wide,
        wide // width + gathered.shape[0],
    )


def back_shapes(tokens, width):
    return [
        shape(tokens, width, dtype=F32),
        shape(tokens, width),
        shape(tokens, width),
        shape(tokens, width),
        shape(tokens, width),
        shape(tokens, width),
        shape(EDGE, width),
    ]


def saved_scratch(saved):
    heads_t, query_t, value8, key_t, attend = saved
    keys = attend.shape[1]
    width = heads_t.shape[0]
    return [pltpu.VMEM(x.shape, x.dtype) for x in saved] + [
        pltpu.VMEM((keys, width), BF16),
        pltpu.VMEM((keys, width), BF16),
        pltpu.VMEM((width, LANES), BF16),
        pltpu.VMEM((2, keys, 2 * LANES), BF16),
    ]


def layer_call(kernel, numbers, small, kept, operands, late, outs, copied, kinds, saved, wide, tokens, limit, extra=()):
    parts, _, _, _, width = kept[0].shape
    return call(
        kernel,
        numbers,
        kept,
        operands,
        [*late, *saved],
        outs,
        [
            *[pltpu.VMEM(x.shape, BF16) for x in feed_shapes(kept[0], wide)],
            squares_scratch(kept[0], 3),
            pltpu.VMEM((tokens, wide), BF16),
            pltpu.VMEM((LANES, width), BF16),
            pltpu.VMEM((tokens, wide), BF16),
            pltpu.VMEM((tokens, width), F32),
            pltpu.VMEM((tokens, width), BF16),
            *[pltpu.VMEM((tokens, width), F32)] * kinds,
            pltpu.VMEM((width, LANES), BF16),
            *saved_scratch(saved),
            *extra,
        ],
        limit,
        8 * tokens * width * wide,
        wide // width + parts + 3 + 4 + PAIRS + 6 + 9,
        small,
        copied,
    )


def input_back(grad_one, query_grad, key_own, value_own, weights, through=()):
    gathered, start = weights
    tokens, width = grad_one.shape
    outs = call(
        input_back_kernel,
        [start, len(through)],
        [gathered],
        [],
        [grad_one, query_grad, key_own, value_own, *through],
        [*through, shape(tokens, width, dtype=F32)],
        [squares_scratch(gathered, 3), pltpu.VMEM((tokens, width), F32), pltpu.VMEM((3, tokens, width), BF16)],
        30,
        1 << 36,
        7,
        (),
        len(through),
        {5 + i: i for i in range(len(through))},
    )
    return outs[-1], *outs[:-1]


def pack(place, w_query, w_key, w_value, w_out, w_up, w_down, each):
    rows, width = w_query.shape[1:]
    return pl.pallas_call(
        pack_kernel,
        out_shape=[shape(each + 2, rows, width), shape(each, rows, width)],
        in_specs=[SMEM] + [ANY] * 6,
        out_specs=[VMEM] * 2,
        scratch_shapes=[pltpu.SemaphoreType.DMA((2 * each + 2,))],
    )(place, w_query, w_key, w_value, w_out, w_up, w_down)


def xor_pairs(count, bit):
    return [(i, i ^ bit) for i in range(count)]


def sum_prefixes(total):
    place = lax.axis_index("keys")
    places = lax.axis_size("keys")
    step = places // 4
    while step:
        split = total.reshape(total.shape[0], 2, -1, total.shape[2])
        mine = (place // step) % 2
        sent = lax.dynamic_index_in_dim(split, 1 - mine, 1, False).astype(BF16)
        kept = lax.dynamic_index_in_dim(split, mine, 1, False)
        total = kept + lax.ppermute(sent, "keys", xor_pairs(places, step)).astype(F32)
        step //= 2
    count = lax.axis_size("rows")
    step = 1
    while step < count:
        total = total + lax.ppermute(total.astype(BF16), "rows", xor_pairs(count, step)).astype(F32)
        step *= 2
    return total


def body(
    activations,
    segments,
    prefix_keys,
    prefix_values,
    w_query,
    w_key,
    w_value,
    w_out,
    w_up,
    ff_bias,
    w_down,
    ln_gain,
    ln_bias,
    cotangent,
):
    _, tokens, width = activations.shape
    wide = w_up.shape[2]
    ratio = wide // width
    places = lax.axis_size("keys")
    parts = lax.axis_size("rows")
    rows = width // parts
    place = lax.axis_index("keys")
    prefix = prefix_keys.shape[1] * places
    first_half = place < places // 2

    each = 2 * ratio // places
    shares = pack(place[None], w_query, w_key, w_value, w_out, w_up, w_down, each)

    def gather(share):
        whole = lax.all_gather(share, ("rows", "keys"), axis=0, tiled=True)
        return whole.reshape(parts, places, share.shape[0], rows, width)

    first, second = gather(shares[0]), gather(shares[1])
    squares = [(first, 0), (first, each + 1)]
    feeds = [(first, 1), (second, 0)]

    def exchange(low):
        near = lax.ppermute(low, "keys", xor_pairs(places, 1))
        across = lax.ppermute(low, "keys", [(1, 2), (2, 1)])
        edge = lax.ppermute(
            jnp.where(first_half, low[tokens - EDGE :], low[:EDGE]), "keys", xor_pairs(places, 2)
        )
        return near, across, edge

    def send_halo(halo):
        across = lax.ppermute(halo[1], "keys", [(1, 2), (2, 1)])
        edge = lax.ppermute(halo[2], "keys", xor_pairs(places, 2))
        near = lax.ppermute(halo[0], "keys", xor_pairs(places, 1))
        return near, across, edge

    line = segments[0]

    def ids(where, start, size):
        return lax.dynamic_slice_in_dim(line, where * tokens + start, size, 0)

    own_ids = ids(place, 0, tokens)
    across_ids = jnp.where(
        (place == 1) | (place == 2), ids(jnp.clip(3 - place, 0, places - 1), 0, tokens), -1
    )
    edge_ids = ids(place ^ 2, jnp.where(first_half, 0, tokens - EDGE), EDGE)
    key_ids = jnp.concatenate([own_ids, ids(place ^ 1, 0, tokens), across_ids, edge_ids])
    allowed = jnp.concatenate([key_ids[:, None] == own_ids[None, :], jnp.ones((prefix, tokens), bool)], 0)
    bias = jnp.pad(jnp.where(allowed, 0.0, MASKED_SCORE).astype(F32), ((0, 0), (0, LANES - tokens)))

    prefixes = lax.all_gather(jnp.stack([prefix_keys, prefix_values]), "keys", axis=2, tiled=True)

    low = activations[0]
    hidden = low.astype(F32)
    kept = []
    for layer in range(LAYERS):
        gains, shifts = ln_gain[layer][:, None], ln_bias[layer][:, None]
        around = exchange(low)
        middle, normed_one, inverse_one, query_t, value8, key_t, attend, heads_t = attention_forward(
            hidden,
            low,
            around,
            bias,
            prefixes[0, layer],
            prefixes[1, layer],
            gains[0],
            shifts[0],
            squares[layer],
        )
        saved = (heads_t, query_t, value8, key_t, attend)
        kept.append(((normed_one, inverse_one), saved))
        if layer < LAYERS - 1:
            hidden, low, *second_norm = feed_forward(middle, ff_bias[layer][None], gains[1], shifts[1], feeds[layer])

    flag = first_half.astype(jnp.int32)[None]
    back = back_shapes(tokens, width)
    both = shape(2, prefix, width, dtype=F32)
    (normed_one, inverse_one), saved = kept[1]
    gains, shifts = ln_gain[1][:, None], ln_bias[1][:, None]
    result, grad_one, query_grad, key_own, value_own, *halo, prefix_after = layer_call(
        last_kernel,
        [feeds[1][1], squares[1][1]],
        (),
        [feeds[1][0], squares[1][0]],
        [middle, ff_bias[1][None], gains[1], shifts[1], cotangent[0], inverse_one, gains[0]],
        [normed_one],
        [shape(tokens, width), *back, both],
        5,
        1,
        saved,
        wide,
        tokens,
        52,
    )
    near, across, edge = send_halo(halo)
    (gradient,) = input_back(grad_one, query_grad, key_own, value_own, squares[1])
    (normed_one, inverse_one), saved = kept[0]
    normed_two, inverse_two, slope = second_norm
    gains = ln_gain[0][:, None]
    half = prefix // 2
    back[-1] = shape(EDGE + LAYERS * 2 * half, width)
    grad_one, query_grad, key_own, value_own, *halo, prefix_kept = layer_call(
        back_kernel,
        [feeds[0][1], squares[0][1]],
        (flag,),
        [feeds[0][0], squares[0][0]],
        [gradient, near, across, edge, inverse_two, gains[1], inverse_one, gains[0], prefix_after],
        [normed_two, slope, normed_one],
        [*back, shape(LAYERS * 2, half, width, dtype=F32)],
        4,
        2,
        saved,
        wide,
        tokens,
        50,
        [pltpu.VMEM(both.shape, F32)],
    )
    near, across, edge = send_halo(halo)
    gradient, prefix_kept = input_back(grad_one, query_grad, key_own, value_own, squares[0], [prefix_kept])
    prefix_total = sum_prefixes(prefix_kept + edge[EDGE:].reshape(LAYERS * 2, half, width).astype(F32))
    prefix_total = prefix_total.reshape(LAYERS, 2, prefix // places, width)
    edge = edge[:EDGE]
    extra = edge.astype(F32)
    lead = jnp.where(first_half, 0.0, extra)
    tail = jnp.where(first_half, extra, 0.0)
    gradient = (
        gradient
        + near.astype(F32)
        + across.astype(F32)
        + jnp.concatenate([lead, jnp.zeros((tokens - 2 * EDGE, width), F32), tail], 0)
    )
    return (
        result[None],
        gradient[None],
        prefix_total[:, 0],
        prefix_total[:, 1],
    )


def solution(mesh):
    placed = (
        P("rows", "keys", None),
        P("rows", None),
        P(None, "keys", None),
        P(None, "keys", None),
        P(None, "rows", None),
        P(None, "rows", None),
        P(None, "rows", None),
        P(None, "rows", None),
        P(None, "rows", None),
        P(),
        P(None, "rows", None),
        P(),
        P(),
        P("rows", "keys", None),
    )
    return jax.shard_map(
        body,
        mesh=mesh,
        in_specs=placed,
        out_specs=(
            P("rows", "keys", None),
            P("rows", "keys", None),
            P(None, "keys", None),
            P(None, "keys", None),
        ),
        check_vma=False,
    )
```

```python
from functools import partial

import jax
import jax.numpy as jnp
import numpy as np
from jax import lax
from jax.experimental import pallas as pl
from jax.experimental.pallas import tpu as pltpu
from jax.sharding import PartitionSpec as P

H = 16
HD = 64
LAYERS = 2
PAIRS = H // 2
EDGE = 32
LANES = 256
NORM_EPSILON = 1e-05
MASKED_SCORE = -1000000000.0
SCORE_SCALE = 0.125
F32 = jnp.float32
BF16 = jnp.bfloat16
MIB = 1 << 20


def nn(a, b):
    return lax.dot_general(a, b, (((1,), (0,)), ((), ())), preferred_element_type=F32)


def nt(a, b):
    return lax.dot_general(a, b, (((1,), (1,)), ((), ())), preferred_element_type=F32)


def ds(start, size):
    return pl.ds(pl.multiple_of(start, size), size)


def layer_norm(hidden, gain, shift):
    centered = hidden - jnp.mean(hidden, -1, keepdims=True)
    inverse = lax.rsqrt(jnp.mean(centered * centered, -1, keepdims=True) + NORM_EPSILON)
    normed = centered * inverse
    return normed * gain + shift, normed, inverse


def norm_back(grad_out, gain, normed, inverse):
    scaled = grad_out * gain
    return inverse * (
        scaled
        - jnp.mean(scaled, -1, keepdims=True)
        - normed * jnp.mean(scaled * normed, -1, keepdims=True)
    )


class Loads:
    def __init__(self, sems):
        self.sems, self.copies, self.count = sems, {}, 0

    def start(self, name, source, target):
        copy = pltpu.make_async_copy(source, target, self.sems.at[self.count])
        copy.start()
        self.copies[name] = copy
        self.count += 1

    def wait(self, *names):
        for name in names:
            if name in self.copies:
                self.copies.pop(name).wait()


def square(ref, columns=slice(None)):
    block = ref[:, :, columns]
    return block.reshape(block.shape[0] * block.shape[1], block.shape[2])


def load_attention(loads, gathered, start, kinds, weights):
    for i, kind in enumerate(kinds):
        loads.start(("square", kind), gathered.at[:, kind, start], weights.at[i])


def load_up(loads, gathered, start, up):
    each = up.shape[0] // (gathered.shape[1] // 2)
    for b in range(up.shape[0]):
        loads.start(("up", b), gathered.at[:, b // each, start + b % each], up.at[b])


def load_down(loads, gathered, start, down):
    half, each = down.shape[1:3]
    for r in range(down.shape[0]):
        loads.start(("down", r), gathered.at[r, pl.ds(half, half), pl.ds(start, each)], down.at[r])


def pair_blocks(half):
    zero = jnp.zeros((HD, LANES), half.dtype)
    return jnp.concatenate(
        [
            jnp.concatenate([half[:HD], zero], 1),
            jnp.concatenate([zero, half[HD:]], 1),
        ],
        0,
    )


def attention_kernel(start, *refs):
    (gathered, own, near, across, edge, residual, bias, prefix_k, prefix_v, gain, shift) = refs[:11]
    (middle, normed, inverse, query_t, value8, key_t, attend, heads_t) = refs[11:19]
    (weights, window, key8, value_t, scores, sems) = refs[19:]
    tokens, width = own.shape
    keys = key8.shape[1]
    loads = Loads(sems)
    load_attention(loads, gathered, start, range(4), weights)
    window[pl.ds(0, tokens)] = own[...]
    window[pl.ds(tokens, tokens)] = near[...]
    window[pl.ds(2 * tokens, tokens)] = across[...]
    window[pl.ds(3 * tokens, EDGE)] = edge[...]
    pad = jnp.zeros((LANES - tokens, 256), BF16)
    for kind in range(3):
        loads.wait(("square", kind))

    def tile(j, carry):
        columns = ds(j * 256, 256)
        query = (SCORE_SCALE * nn(own[...], square(weights.at[0], columns))).astype(BF16)
        query_t[columns, :] = jnp.concatenate([query, pad], 0).T
        for kind, prefix, split, turned in ((1, prefix_k, key8, key_t), (2, prefix_v, value8, value_t)):
            local = nn(window[...], square(weights.at[kind], columns)).astype(BF16)
            whole = jnp.concatenate([local, prefix[:, columns]], 0)
            split[2 * j] = whole[:, :128]
            split[2 * j + 1] = whole[:, 128:]
            turned[columns, :] = whole.T
        return carry

    lax.fori_loop(0, width // 256, tile, 0, unroll=2)
    wide = jnp.zeros((1, 2 * LANES), F32)
    step = 128

    def pair(p, carry):
        blocks = pair_blocks(query_t[ds(p * 128, 128), :])
        top = wide + 2 * MASKED_SCORE
        for c in range(0, keys, step):
            part = nn(key8[p, pl.ds(c, step), :], blocks)
            mask = bias[pl.ds(c, step), :]
            part = part + jnp.concatenate([mask, mask], 1)
            scores[pl.ds(c, step), :] = part
            top = jnp.maximum(top, jnp.max(part, 0, keepdims=True))
        total = wide
        for c in range(0, keys, step):
            part = jnp.exp(scores[pl.ds(c, step), :] - top)
            scores[pl.ds(c, step), :] = part
            total = total + jnp.sum(part, 0, keepdims=True)
        scale = 1.0 / total
        for c in range(0, keys, step):
            attend[p, pl.ds(c, step), :] = (scores[pl.ds(c, step), :] * scale).astype(BF16)
        for half in range(2):
            rows = pl.ds(pl.multiple_of(p * 128 + half * HD, HD), HD)
            heads_t[rows, :] = nn(value_t[rows, :], attend[p, :, pl.ds(half * LANES, LANES)])
        return carry

    lax.fori_loop(0, PAIRS, pair, 0)
    loads.wait(("square", 3))
    heads = heads_t[...].astype(BF16).T[:tokens]
    for c in range(0, width, 512):
        columns = pl.ds(c, 512)
        middle[:, columns] = residual[:, columns] + nn(heads, square(weights.at[3], columns))
    result, n, r = layer_norm(middle[...], gain[...], shift[...])
    middle[...] = result
    normed[...] = n
    inverse[...] = r


def feed_forward_steps(loads, middle, up_bias, gain, shift, up, down, low, hidden, slope, output):
    tokens, width = middle.shape
    low[pl.ds(0, tokens), :] = middle[...].astype(BF16)
    for b in range(up.shape[0]):
        loads.wait(("up", b))
        for c in range(0, width, 512):
            place = pl.ds(b * width + c, 512)
            u = nn(low[pl.ds(0, tokens), :], square(up.at[b], pl.ds(c, 512))) + up_bias[:, place]
            part = 0.5 + 0.5 * lax.erf(u * (0.5**0.5))
            hidden[:, place] = (u * part).astype(BF16)
            slope[:, place] = (part + u * (jnp.exp(-0.5 * u * u) * ((2 * np.pi) ** -0.5))).astype(BF16)
    for r in range(down.shape[0]):
        loads.wait(("down", r))
    for c in range(0, width, 512):
        columns = pl.ds(c, 512)
        block = down[:, :, :, :, columns].reshape(hidden.shape[1], 512)
        output[:, columns] = middle[:, columns] + nn(hidden[...], block)
    return layer_norm(output[...], gain[...], shift[...])


def forward_kernel(start, *refs):
    (gathered, middle, up_bias, gain, shift) = refs[:5]
    (output, low, normed, inverse, slope) = refs[5:10]
    (up, down, hidden, sems) = refs[10:]
    loads = Loads(sems)
    load_up(loads, gathered, start, up)
    load_down(loads, gathered, start, down)
    result, n, r = feed_forward_steps(loads, middle, up_bias, gain, shift, up, down, low, hidden, slope, output)
    output[...] = result
    low[...] = result.astype(BF16)
    normed[...] = n
    inverse[...] = r


def feed_back_steps(loads, grad_two, slope, normed_one, inverse_one, gain_one, up, down, weights, low, hidden, grad_one, heads_grad, grad_out):
    tokens, width = grad_two.shape
    low[pl.ds(0, tokens), :] = grad_two.astype(BF16)
    grad_one[...] = grad_two
    size = hidden.shape[1] // down.shape[0]
    for r in range(down.shape[0]):
        loads.wait(("down", r))
        place = pl.ds(r * size, size)
        back = nt(low[pl.ds(0, tokens), :], down[r].reshape(size, width))
        hidden[:, place] = (back * slope[:, place].astype(F32)).astype(BF16)
    rows = up.shape[2]
    for b in range(0, up.shape[0], 2):
        loads.wait(("up", b), ("up", b + 1))
        for c in range(0, width, 512):
            total = grad_one[:, pl.ds(c, 512)]
            for i in (b, b + 1):
                block = up[i, pl.ds(c // rows, 512 // rows)].reshape(512, width)
                total = total + nt(hidden[:, pl.ds(i * width, width)], block)
            grad_one[:, pl.ds(c, 512)] = total
    loads.wait("normed_one")
    back = norm_back(grad_one[...], gain_one[...], normed_one[...], inverse_one[...])
    grad_one[...] = back
    loads.start("grad_out", grad_one, grad_out)
    low[pl.ds(0, tokens), :] = back.astype(BF16)
    low[pl.ds(tokens, LANES - tokens), :] = jnp.zeros((LANES - tokens, width), BF16)
    loads.wait(("square", 3))
    heads_grad[...] = nt(square(weights.at[0]), low[...]).astype(BF16)


def attention_back_steps(loads, heads_grad, heads_t, query_t, value8, key_t, attend, weights, key_grad, value_grad, query_grad_t, query_rows, steps, outs):
    (query_grad, key_own, value_own, near_grad, across_grad, edge_grad, prefix_grad) = outs
    tokens, width = query_rows.shape
    keys = attend.shape[1]
    span = keys - prefix_grad.shape[1]
    loads.wait("low_out")
    loads.wait("heads_t", "query_t", "value8", "key_t")
    step = 128
    for p in range(PAIRS):
        loads.wait(("attend", p))
        rows = pl.ds(p * 128, 128)
        grad_t = heads_grad[rows, :]
        product = grad_t.astype(F32) * heads_t[rows, :]
        dots = jnp.concatenate(
            [jnp.sum(product[:HD], 0, keepdims=True), jnp.sum(product[HD:], 0, keepdims=True)], 1
        )
        blocks = pair_blocks(grad_t)
        grad_v = nt(attend[p], blocks)
        value_grad[:, rows] = grad_v.astype(BF16)
        prefix_grad[1, :, rows] = grad_v[span:]
        here = steps.at[p % 2]
        for c in range(0, keys, step):
            part = nn(value8[p, pl.ds(c, step), :], blocks) - dots
            here[pl.ds(c, step), :] = (attend[p, pl.ds(c, step), :].astype(F32) * part).astype(BF16)
        grad_k = nt(here[...], pair_blocks(query_t[rows, :]))
        key_grad[:, rows] = grad_k.astype(BF16)
        prefix_grad[0, :, rows] = grad_k[span:]
        for half in range(2):
            place = pl.ds(p * 128 + half * HD, HD)
            query_grad_t[place, :] = nn(key_t[place, :], here[:, pl.ds(half * LANES, LANES)]).astype(BF16)
    query_rows[...] = query_grad_t[...].T[:tokens]
    loads.start("query_out", query_rows, query_grad)
    loads.start("key_out", key_grad.at[pl.ds(0, tokens)], key_own)
    loads.start("value_out", value_grad.at[pl.ds(0, tokens)], value_own)
    loads.wait(("square", 1), ("square", 2))
    outer = pl.ds(tokens, span - tokens)
    rows = weights.shape[2]
    for c in range(0, width, 512):
        part = pl.ds(c // rows, 512 // rows)
        outer_grad = (
            nt(key_grad[outer, :], weights[1, part].reshape(512, width))
            + nt(value_grad[outer, :], weights[2, part].reshape(512, width))
        ).astype(BF16)
        near_grad[:, pl.ds(c, 512)] = outer_grad[:tokens]
        across_grad[:, pl.ds(c, 512)] = outer_grad[tokens : 2 * tokens]
        edge_grad[pl.ds(0, EDGE), pl.ds(c, 512)] = outer_grad[2 * tokens :]
    loads.wait("grad_out", "query_out", "key_out", "value_out")


def load_saved(loads, gathered, start, saved, weights, buffers):
    load_attention(loads, gathered, start, [3], weights.at[pl.ds(0, 1)])
    for name, source, target in zip(("heads_t", "query_t", "value8", "key_t"), saved, buffers):
        loads.start(name, source, target)
    for p in range(PAIRS):
        loads.start(("attend", p), saved[4].at[p], buffers[4].at[p])
    load_attention(loads, gathered, start, [1, 2], weights.at[pl.ds(1, 2)])


def input_back_steps(loads, weights, grad_one, sides, grad_input):
    width = grad_one.shape[1]
    rows = weights.shape[2]
    for kind in range(3):
        loads.wait(("side", kind), ("square", kind))
        before = grad_one if kind == 0 else grad_input
        for c in range(0, width, 512):
            columns = pl.ds(c, 512)
            part = nt(sides[kind], weights[kind, pl.ds(c // rows, 512 // rows)].reshape(512, width))
            grad_input[:, columns] = before[:, columns] + (SCORE_SCALE * part if kind == 0 else part)


def last_kernel(feed_start, attention_start, *refs):
    (feed, squares, middle, up_bias, gain_two, shift_two, cotangent, inverse_one, gain_one) = refs[:9]
    normed_hbm, saved = refs[9], refs[10:15]
    low_out, grad_out = refs[15:17]
    outs = refs[17:24]
    (up, down, weights, slope, low, hidden, grad_one, query_rows, normed_one, heads_grad) = refs[24:34]
    buffers = refs[34:39]
    (key_grad, value_grad, query_grad_t, steps, sems) = refs[39:]
    loads = Loads(sems)
    load_up(loads, feed, feed_start, up)
    load_down(loads, feed, feed_start, down)
    loads.start("normed_one", normed_hbm, normed_one)
    load_saved(loads, squares, attention_start, saved, weights, buffers)
    result, n, r = feed_forward_steps(
        loads, middle, up_bias, gain_two, shift_two, up, down, low, hidden, slope, grad_one
    )
    query_rows[...] = result.astype(BF16)
    loads.start("low_out", query_rows, low_out)
    grad_two = norm_back(cotangent[...].astype(F32), gain_two[...], n, r)
    feed_back_steps(
        loads, grad_two, slope, normed_one, inverse_one, gain_one, up, down, weights, low, hidden, grad_one, heads_grad, grad_out
    )
    attention_back_steps(
        loads, heads_grad, *buffers[:5], weights, key_grad, value_grad, query_grad_t, query_rows, steps, outs
    )


def back_kernel(feed_start, attention_start, *refs):
    (flag, feed, squares) = refs[:3]
    (grad, near, across, edge, inverse_two, gain_two, inverse_one, gain_one, prefix_after) = refs[3:12]
    (normed_two_hbm, slope_hbm, normed_one_hbm) = refs[12:15]
    saved = refs[15:20]
    grad_out = refs[20]
    outs = refs[21:27]
    edge_grad, prefix_kept = refs[26:28]
    (up, down, weights, slope, low, hidden, grad_one, query_rows, normed_two, normed_one, heads_grad) = refs[28:39]
    buffers = refs[39:44]
    (key_grad, value_grad, query_grad_t, steps, prefix_grad, sems) = refs[44:]
    tokens, width = grad_one.shape
    loads = Loads(sems)
    loads.start("normed_two", normed_two_hbm, normed_two)
    loads.start("slope", slope_hbm, slope)
    load_down(loads, feed, feed_start, down)
    load_up(loads, feed, feed_start, up)
    loads.start("normed_one", normed_one_hbm, normed_one)
    load_saved(loads, squares, attention_start, saved, weights, buffers)
    grad_one[...] = grad[...] + near[...].astype(F32) + across[...].astype(F32)
    last = flag[0].astype(F32)
    extra = edge[...].astype(F32)
    head, tail = pl.ds(0, EDGE), pl.ds(tokens - EDGE, EDGE)
    grad_one[head, :] = grad_one[head, :] + extra * (1.0 - last)
    grad_one[tail, :] = grad_one[tail, :] + extra * last
    loads.wait("normed_two")
    grad_two = norm_back(grad_one[...], gain_two[...], normed_two[...], inverse_two[...])
    loads.wait("slope")
    feed_back_steps(
        loads, grad_two, slope, normed_one, inverse_one, gain_one, up, down, weights, low, hidden, grad_one, heads_grad, grad_out
    )
    attention_back_steps(
        loads, heads_grad, *buffers[:5], weights, key_grad, value_grad, query_grad_t, query_rows, steps, (*outs, prefix_grad)
    )
    half = prefix_kept.shape[1]
    mine = 1 - flag[0]
    for layer, part in enumerate((prefix_grad, prefix_after)):
        for i in range(2):
            at = 2 * layer + i
            prefix_kept[at] = part[i, ds(mine * half, half), :]
            edge_grad[pl.ds(EDGE + at * half, half), :] = part[i, ds((1 - mine) * half, half), :].astype(BF16)


def input_back_kernel(start, through, *refs):
    (gathered, grad_hbm, query_hbm, key_hbm, value_hbm) = refs[:5]
    (grad_input, weights, grad_one, sides, sems) = refs[5 + 2 * through :]
    loads = Loads(sems)
    loads.start("grad", grad_hbm, grad_one)
    for kind, source in enumerate((query_hbm, key_hbm, value_hbm)):
        loads.start(("side", kind), source, sides.at[kind])
        load_attention(loads, gathered, start, [kind], weights.at[pl.ds(kind, 1)])
    loads.wait("grad")
    input_back_steps(loads, weights, grad_one, sides, grad_input)


def pack_kernel(place, query, key, value, out, up, down, first, second, sems):
    places = 4
    half = places // 2
    rows = query.shape[1]
    width = query.shape[2]
    each = second.shape[0]
    for k in range(places):

        @pl.when(place[0] == k)
        def _():
            matrix = (query, key, value, out)[k]
            jobs = [(matrix.at[0], first.at[0]), (matrix.at[1], first.at[each + 1])]
            for layer, target, begin in ((0, first, 1), (1, second, 0)):
                for i in range(each):
                    b = k * each + i
                    if k < half:
                        source = up.at[layer, :, pl.ds(b * width, width)]
                    else:
                        source = down.at[layer, pl.ds((b - half * each) * rows, rows)]
                    jobs.append((source, target.at[begin + i]))
            copies = [pltpu.make_async_copy(a, b, sems.at[i]) for i, (a, b) in enumerate(jobs)]
            for copy in copies:
                copy.start()
            for copy in copies:
                copy.wait()


VMEM = pl.BlockSpec(memory_space=pltpu.VMEM)
SMEM = pl.BlockSpec(memory_space=pltpu.SMEM)
ANY = pl.BlockSpec(memory_space=pl.ANY)
HBM = pl.BlockSpec(memory_space=pltpu.HBM)


def call(kernel, numbers, kept, operands, late, outs, scratch, limit, flops, sem_count, small=(), copied=0, aliases={}):
    moved = sum(x.size * x.dtype.itemsize for x in (*operands, *late)) + 16 * MIB
    return pl.pallas_call(
        partial(kernel, *numbers),
        out_shape=[shape(*x.shape, dtype=x.dtype) for x in outs],
        input_output_aliases=aliases,
        in_specs=[SMEM] * len(small) + [ANY] * len(kept) + [VMEM] * len(operands) + [ANY] * len(late),
        out_specs=[HBM] * copied + [VMEM] * (len(outs) - copied),
        scratch_shapes=[*scratch, pltpu.SemaphoreType.DMA((sem_count,))],
        compiler_params=pltpu.CompilerParams(vmem_limit_bytes=limit * MIB),
        cost_estimate=pl.CostEstimate(flops=flops, bytes_accessed=moved, transcendentals=0),
    )(*small, *kept, *operands, *late)


def shape(*sizes, dtype=BF16):
    return jax.ShapeDtypeStruct(sizes, dtype)


def feed_shapes(gathered, wide):
    parts, places, _, rows, width = gathered.shape
    ratio = wide // width
    return [shape(ratio, parts, rows, width), shape(parts, places // 2, 2 * ratio // places, rows, width)]


def squares_scratch(gathered, count):
    parts, _, _, rows, width = gathered.shape
    return pltpu.VMEM((count, parts, rows, width), BF16)


def attention_forward(inputs, inputs_low, around, bias, prefix_k, prefix_v, gain, shift, weights):
    gathered, start = weights
    tokens, width = inputs.shape
    keys = bias.shape[0]
    span = keys - prefix_k.shape[0]
    return call(
        attention_kernel,
        [start],
        [gathered],
        [inputs_low, *around, inputs, bias, prefix_k, prefix_v, gain, shift],
        [],
        [
            shape(tokens, width, dtype=F32),
            shape(tokens, width, dtype=F32),
            shape(tokens, 1, dtype=F32),
            shape(width, LANES),
            shape(PAIRS, keys, 128),
            shape(width, keys),
            shape(PAIRS, keys, 2 * LANES),
            shape(width, LANES, dtype=F32),
        ],
        [
            squares_scratch(gathered, 4),
            pltpu.VMEM((span, width), BF16),
            pltpu.VMEM((PAIRS, keys, 128), BF16),
            pltpu.VMEM((width, keys), BF16),
            pltpu.VMEM((keys, 2 * LANES), F32),
        ],
        40,
        2 * tokens * width * width * 8,
        4,
    )


def feed_forward(middle, up_bias, gain, shift, weights):
    gathered, start = weights
    tokens, width = middle.shape
    wide = up_bias.shape[1]
    return call(
        forward_kernel,
        [start],
        [gathered],
        [middle, up_bias, gain, shift],
        [],
        [
            shape(tokens, width, dtype=F32),
            shape(tokens, width),
            shape(tokens, width, dtype=F32),
            shape(tokens, 1, dtype=F32),
            shape(tokens, wide),
        ],
        [*[pltpu.VMEM(x.shape, BF16) for x in feed_shapes(gathered, wide)], pltpu.VMEM((tokens, wide), BF16)],
        40,
        4 * tokens * width * wide,
        wide // width + gathered.shape[0],
    )


def back_shapes(tokens, width):
    return [
        shape(tokens, width, dtype=F32),
        shape(tokens, width),
        shape(tokens, width),
        shape(tokens, width),
        shape(tokens, width),
        shape(tokens, width),
        shape(EDGE, width),
    ]


def saved_scratch(saved):
    heads_t, query_t, value8, key_t, attend = saved
    keys = attend.shape[1]
    width = heads_t.shape[0]
    return [pltpu.VMEM(x.shape, x.dtype) for x in saved] + [
        pltpu.VMEM((keys, width), BF16),
        pltpu.VMEM((keys, width), BF16),
        pltpu.VMEM((width, LANES), BF16),
        pltpu.VMEM((2, keys, 2 * LANES), BF16),
    ]


def layer_call(kernel, numbers, small, kept, operands, late, outs, copied, kinds, saved, wide, tokens, limit, extra=()):
    parts, _, _, _, width = kept[0].shape
    return call(
        kernel,
        numbers,
        kept,
        operands,
        [*late, *saved],
        outs,
        [
            *[pltpu.VMEM(x.shape, BF16) for x in feed_shapes(kept[0], wide)],
            squares_scratch(kept[0], 3),
            pltpu.VMEM((tokens, wide), BF16),
            pltpu.VMEM((LANES, width), BF16),
            pltpu.VMEM((tokens, wide), BF16),
            pltpu.VMEM((tokens, width), F32),
            pltpu.VMEM((tokens, width), BF16),
            *[pltpu.VMEM((tokens, width), F32)] * kinds,
            pltpu.VMEM((width, LANES), BF16),
            *saved_scratch(saved),
            *extra,
        ],
        limit,
        8 * tokens * width * wide,
        wide // width + parts + 3 + 4 + PAIRS + 6 + 9,
        small,
        copied,
    )


def input_back(grad_one, query_grad, key_own, value_own, weights, through=()):
    gathered, start = weights
    tokens, width = grad_one.shape
    outs = call(
        input_back_kernel,
        [start, len(through)],
        [gathered],
        [],
        [grad_one, query_grad, key_own, value_own, *through],
        [*through, shape(tokens, width, dtype=F32)],
        [squares_scratch(gathered, 3), pltpu.VMEM((tokens, width), F32), pltpu.VMEM((3, tokens, width), BF16)],
        30,
        6 * tokens * width * width,
        7,
        (),
        len(through),
        {5 + i: i for i in range(len(through))},
    )
    return outs[-1], *outs[:-1]


def pack(place, w_query, w_key, w_value, w_out, w_up, w_down, each):
    rows, width = w_query.shape[1:]
    return pl.pallas_call(
        pack_kernel,
        out_shape=[shape(each + 2, rows, width), shape(each, rows, width)],
        in_specs=[SMEM] + [ANY] * 6,
        out_specs=[VMEM] * 2,
        scratch_shapes=[pltpu.SemaphoreType.DMA((2 * each + 2,))],
    )(place, w_query, w_key, w_value, w_out, w_up, w_down)


def xor_pairs(count, bit):
    return [(i, i ^ bit) for i in range(count)]


def sum_prefixes(total):
    place = lax.axis_index("keys")
    places = lax.axis_size("keys")
    step = places // 4
    while step:
        split = total.reshape(total.shape[0], 2, -1, total.shape[2])
        mine = (place // step) % 2
        sent = lax.dynamic_index_in_dim(split, 1 - mine, 1, False).astype(BF16)
        kept = lax.dynamic_index_in_dim(split, mine, 1, False)
        total = kept + lax.ppermute(sent, "keys", xor_pairs(places, step)).astype(F32)
        step //= 2
    count = lax.axis_size("rows")
    step = count // 2
    while step:
        total = total + lax.ppermute(total.astype(BF16), "rows", xor_pairs(count, step)).astype(F32)
        step //= 2
    return total


def body(
    activations,
    segments,
    prefix_keys,
    prefix_values,
    w_query,
    w_key,
    w_value,
    w_out,
    w_up,
    ff_bias,
    w_down,
    ln_gain,
    ln_bias,
    cotangent,
):
    _, tokens, width = activations.shape
    wide = w_up.shape[2]
    ratio = wide // width
    places = lax.axis_size("keys")
    parts = lax.axis_size("rows")
    rows = width // parts
    place = lax.axis_index("keys")
    prefix = prefix_keys.shape[1] * places
    first_half = place < places // 2

    each = 2 * ratio // places
    shares = pack(place[None], w_query, w_key, w_value, w_out, w_up, w_down, each)

    def gather(share):
        whole = lax.all_gather(share, ("rows", "keys"), axis=0, tiled=True)
        return whole.reshape(parts, places, share.shape[0], rows, width)

    first, second = gather(shares[0]), gather(shares[1])
    squares = [(first, 0), (first, each + 1)]
    feeds = [(first, 1), (second, 0)]

    def exchange(low):
        near = lax.ppermute(low, "keys", xor_pairs(places, 1))
        across = lax.ppermute(low, "keys", [(1, 2), (2, 1)])
        edge = lax.ppermute(
            jnp.where(first_half, low[tokens - EDGE :], low[:EDGE]), "keys", xor_pairs(places, 2)
        )
        return near, across, edge

    def send_halo(halo):
        near = lax.ppermute(halo[0], "keys", xor_pairs(places, 1))
        across = lax.ppermute(halo[1], "keys", [(1, 2), (2, 1)])
        edge = lax.ppermute(halo[2], "keys", xor_pairs(places, 2))
        return near, across, edge

    line = segments[0]

    def ids(where, start, size):
        return lax.dynamic_slice_in_dim(line, where * tokens + start, size, 0)

    own_ids = ids(place, 0, tokens)
    across_ids = jnp.where(
        (place == 1) | (place == 2), ids(jnp.clip(3 - place, 0, places - 1), 0, tokens), -1
    )
    edge_ids = ids(place ^ 2, jnp.where(first_half, 0, tokens - EDGE), EDGE)
    key_ids = jnp.concatenate([own_ids, ids(place ^ 1, 0, tokens), across_ids, edge_ids])
    allowed = jnp.concatenate([key_ids[:, None] == own_ids[None, :], jnp.ones((prefix, tokens), bool)], 0)
    bias = jnp.pad(jnp.where(allowed, 0.0, MASKED_SCORE).astype(F32), ((0, 0), (0, LANES - tokens)))

    prefixes = lax.all_gather(jnp.stack([prefix_keys, prefix_values]), "keys", axis=2, tiled=True)

    low = activations[0]
    hidden = low.astype(F32)
    kept = []
    for layer in range(LAYERS):
        gains, shifts = ln_gain[layer][:, None], ln_bias[layer][:, None]
        around = exchange(low)
        middle, normed_one, inverse_one, query_t, value8, key_t, attend, heads_t = attention_forward(
            hidden,
            low,
            around,
            bias,
            prefixes[0, layer],
            prefixes[1, layer],
            gains[0],
            shifts[0],
            squares[layer],
        )
        saved = (heads_t, query_t, value8, key_t, attend)
        kept.append(((normed_one, inverse_one), saved))
        if layer < LAYERS - 1:
            hidden, low, *second_norm = feed_forward(middle, ff_bias[layer][None], gains[1], shifts[1], feeds[layer])

    flag = first_half.astype(jnp.int32)[None]
    back = back_shapes(tokens, width)
    both = shape(2, prefix, width, dtype=F32)
    (normed_one, inverse_one), saved = kept[1]
    gains, shifts = ln_gain[1][:, None], ln_bias[1][:, None]
    result, grad_one, query_grad, key_own, value_own, *halo, prefix_after = layer_call(
        last_kernel,
        [feeds[1][1], squares[1][1]],
        (),
        [feeds[1][0], squares[1][0]],
        [middle, ff_bias[1][None], gains[1], shifts[1], cotangent[0], inverse_one, gains[0]],
        [normed_one],
        [shape(tokens, width), *back, both],
        5,
        1,
        saved,
        wide,
        tokens,
        52,
    )
    near, across, edge = send_halo(halo)
    (gradient,) = input_back(grad_one, query_grad, key_own, value_own, squares[1])
    (normed_one, inverse_one), saved = kept[0]
    normed_two, inverse_two, slope = second_norm
    gains = ln_gain[0][:, None]
    half = prefix // 2
    back[-1] = shape(EDGE + LAYERS * 2 * half, width)
    grad_one, query_grad, key_own, value_own, *halo, prefix_kept = layer_call(
        back_kernel,
        [feeds[0][1], squares[0][1]],
        (flag,),
        [feeds[0][0], squares[0][0]],
        [gradient, near, across, edge, inverse_two, gains[1], inverse_one, gains[0], prefix_after],
        [normed_two, slope, normed_one],
        [*back, shape(LAYERS * 2, half, width, dtype=F32)],
        4,
        2,
        saved,
        wide,
        tokens,
        50,
        [pltpu.VMEM(both.shape, F32)],
    )
    near, across, edge = send_halo(halo)
    gradient, prefix_kept = input_back(grad_one, query_grad, key_own, value_own, squares[0], [prefix_kept])
    prefix_total = sum_prefixes(prefix_kept + edge[EDGE:].reshape(LAYERS * 2, half, width).astype(F32))
    prefix_total = prefix_total.reshape(LAYERS, 2, prefix // places, width)
    edge = edge[:EDGE]
    extra = edge.astype(F32)
    lead = jnp.where(first_half, 0.0, extra)
    tail = jnp.where(first_half, extra, 0.0)
    gradient = (
        gradient
        + near.astype(F32)
        + across.astype(F32)
        + jnp.concatenate([lead, jnp.zeros((tokens - 2 * EDGE, width), F32), tail], 0)
    )
    return (
        result[None],
        gradient[None],
        prefix_total[:, 0],
        prefix_total[:, 1],
    )


def solution(mesh):
    placed = (
        P("rows", "keys", None),
        P("rows", None),
        P(None, "keys", None),
        P(None, "keys", None),
        P(None, "rows", None),
        P(None, "rows", None),
        P(None, "rows", None),
        P(None, "rows", None),
        P(None, "rows", None),
        P(),
        P(None, "rows", None),
        P(),
        P(),
        P("rows", "keys", None),
    )
    return jax.shard_map(
        body,
        mesh=mesh,
        in_specs=placed,
        out_specs=(
            P("rows", "keys", None),
            P("rows", "keys", None),
            P(None, "keys", None),
            P(None, "keys", None),
        ),
        check_vma=False,
    )
```
